256 devices in a mesh: caption: 16 (over y_lo, z), replica: 16 (over x, y_hi, core).
Axes of the slice: x: 4, y: 4 (y_hi: 2, y_lo: 2; y = y_hi * 2 + y_lo), z: 8, core: 2. Of those that a mesh axis runs over, the one named last changes fastest.
Arguments:
- caption_feats: bfloat16 [16, 2048, 1152], P('replica', 'caption')
- text_head: bfloat16 [1152, 1152], replicated, may hold values from -0.1875 to 0.1875
- image_pool: bfloat16 [16, 2048, 1152], P('caption', 'replica')
- image_head: bfloat16 [1152, 1152], replicated, may hold values from -0.1875 to 0.1875
- image_owner: int32 [16, 1536, 1], P(None, 'caption'), may hold values from 0 to 15; in each aligned block of 96 rows (0 to 95, 96 to 191, ..., all dimensions but the last counted through in order) at most 12 rows name the same one
- image_slot: int32 [16, 1536], P(None, 'caption'), may hold values from 0 to 127
- caption_image: int32 [16, 2048], P('replica', 'caption'), may hold values from 0 to 95
- logit_scale: float32 [1], replicated, may hold values from 90 to 130
- logit_bias: float32 [1], replicated, may hold values from -14 to -10
Outputs:
- text_feat_grad: bfloat16 [16, 2048, 1152], P('replica', 'caption')
- pool_grad: bfloat16 [16, 2048, 1152], P('caption', 'replica')
- head_grads: float32 [2304, 1152], P(('caption', 'replica'))
The draws below stay inside these ranges and needn't reach their ends.
Inputs may be any that keep to these rules, and one draw needn't show every extreme that they name: `image_owner`: among the 96 images of one device (aligned blocks of rows in group order), at most 12 have the same owner, and in every draw some owner holds exactly 12 images of some device.
All inputs are finite; a program needn't handle non-finite values.
Results may differ from the reference program's by a relative error of at most 0.0083.
Values may be sent and summed in bfloat16 or wider, within the bound.
No kernel may reach another device: no remote copies, remote signals or barrier semaphores. Data moves between devices by JAX's collectives and lax.ppermute only.
A program may use at most 128 MiB of HBM per device.

```python
import math
import jax
import jax.numpy as jnp
import numpy as np
from jax import lax

D = 1152
EMB = 1152
TXT_DEV = 128
IMG_DEV = 96
POOL_DEV = 128
CAP = 12
CAPTIONS = 2048
IMAGES = 1536
N_CAPTION = 16
N_REPLICA = 16


def neighbour_columns():
    device_total = N_CAPTION * N_REPLICA
    rows_each = 2 * D // device_total
    group_ids = jnp.arange(N_REPLICA, dtype=jnp.int32)[:, None, None]
    block_ids = (jnp.arange(N_CAPTION * TXT_DEV, dtype=jnp.int32) // TXT_DEV)[None, :, None]
    device_ids = block_ids * N_REPLICA + group_ids
    column_ids = jnp.arange(D, dtype=jnp.int32)[None, None, :]
    marked = jnp.zeros((N_REPLICA, N_CAPTION * TXT_DEV, D), jnp.float32)
    for step_off in [device_total - 1, 1, device_total // 2]:
        target = (device_ids + step_off) % device_total
        lower = target * rows_each // 2
        upper = ((target + 1) * rows_each - 1) // 2
        inside = jnp.logical_and(column_ids >= lower, column_ids <= upper)
        marked = jnp.maximum(marked, inside.astype(jnp.float32))
    return 1.0 + 11.0 * marked


def draw_caption_feats(key, part):
    key = jax.random.fold_in(key, 11)
    key_base, key_rows, key_cols = jax.random.split(key, 3)
    full_shape = (N_REPLICA, N_CAPTION * TXT_DEV, D)
    base_draw = jax.random.normal(key_base, full_shape, jnp.float32)
    top_scale = 10.0
    row_scale = jnp.exp(jax.random.uniform(key_rows, (N_REPLICA, N_CAPTION * TXT_DEV, 1), jnp.float32, 0.0, math.log(top_scale)))
    col_scale = jnp.exp(jax.random.uniform(key_cols, (D,), jnp.float32, 0.0, math.log(10.0)))
    return (base_draw * row_scale * col_scale * neighbour_columns() / 3.0).astype(jnp.bfloat16)


def draw_image_pool(key, part):
    key = jax.random.fold_in(key, 23)
    key_base, key_rows, key_cols = jax.random.split(key, 3)
    full_shape = (N_CAPTION, N_REPLICA * POOL_DEV, D)
    base_draw = jax.random.normal(key_base, full_shape, jnp.float32)
    top_scale = 10.0
    row_scale = jnp.exp(jax.random.uniform(key_rows, (N_CAPTION, N_REPLICA * POOL_DEV, 1), jnp.float32, 0.0, math.log(top_scale)))
    col_scale = jnp.exp(jax.random.uniform(key_cols, (D,), jnp.float32, 0.0, math.log(10.0)))
    return (base_draw * row_scale * col_scale / 3.0).astype(jnp.bfloat16)


def plant(array, stream_key, smallest, largest):
    place = [jax.random.randint(jax.random.fold_in(stream_key, axis), (), 0, length) for axis, length in enumerate(array.shape)]
    longest = array.shape.index(max(array.shape))
    next_to = place[:longest] + [(place[longest] + 1) % array.shape[longest]] + place[longest + 1:]
    return array.at[tuple(place)].set(smallest).at[tuple(next_to)].set(largest)


def deal_out(stream_key, own, number, rows, number_of, top, limit, skew):
    sequence = jax.random.permutation(stream_key, number_of)
    heavy_load, ordinary = portions_of(number_of, rows * top, limit, skew, True), portions_of(number_of, rows * top, limit, skew, False)
    places = jnp.arange(number_of)

    def named(lengths, rotation):
        used = int((lengths > 0).sum())
        fixed = max(1, used // 4)
        passed = fixed + (places - fixed + rotation * (used - fixed)) % max(1, number_of - fixed)
        return jnp.zeros((number_of,), jnp.int32).at[sequence[jnp.where(places < fixed, places, passed)]].set(jnp.asarray(lengths, jnp.int32))

    lengths = jnp.where(number % 4 == 0, named(heavy_load, number // 4), named(ordinary, number - number // 4 - 1))
    mixed = jax.random.permutation(jax.random.fold_in(own, 3), number_of)
    source_of, receiver = mixed[0:number_of // 2 * 2:2], mixed[1:number_of // 2 * 2:2]
    room = jnp.minimum(lengths[source_of] - 1, limit - lengths[receiver]) // 2
    room = jnp.where((source_of == sequence[0]) | (receiver == sequence[0]) | (lengths[receiver] == 0), 0, jnp.maximum(room, 0))
    passed = jax.random.randint(jax.random.fold_in(own, 4), (number_of // 2,), 0, 1 << 20) % (room + 1)
    lengths = lengths.at[source_of].add(-passed).at[receiver].add(passed)
    labels = jnp.searchsorted(jnp.cumsum(lengths), jnp.arange(rows * top), side="right").astype(jnp.int32)
    listing = labels.reshape(top, rows).T
    listing = listing[jax.random.permutation(jax.random.fold_in(own, 1), rows)]
    rotation = jax.random.randint(jax.random.fold_in(own, 2), (rows, 1), 0, top)
    return jnp.take_along_axis(listing, (jnp.arange(top)[None, :] + rotation) % top, axis=1)


def portions_of(number_of, total, most, skew, full):
    weights = [(1 << 20) // math.isqrt(standing ** skew) + 1 for standing in range(1, number_of + 1)]
    largest = most if full else min(most, max(-(-total // number_of), total * weights[0] // sum(weights)))
    least = 1 if total - largest >= number_of - 1 else 0
    holding, spare = [largest] + [least] * (number_of - 1), total - largest - least * (number_of - 1)
    while spare > 0:
        movable = [i for i in range(1, number_of) if holding[i] < largest] or [i for i in range(1, number_of) if holding[i] < most]
        whole, left = sum([weights[i] for i in movable]), spare
        for i in movable:
            extra = min(most - holding[i], max(1, left * weights[i] // whole), spare)
            holding[i] = holding[i] + extra
            spare = spare - extra
    return np.array(holding)


def gaussian(own_key, extent, deviation, bound, kind=jnp.bfloat16):
    entries = jax.random.normal(own_key, extent, jnp.float32) * deviation
    return jnp.minimum(jnp.maximum(entries, -bound), bound).astype(kind)


def setup_inputs(seed: int = 0) -> dict:
    key_of = jax.random.split(jax.random.key(seed), 10)
    caption_feats = draw_caption_feats(jax.random.fold_in(key_of[9], 71), 0)
    text_head = gaussian(key_of[1], (D, EMB), D ** -0.5, 0.1875)
    image_pool = draw_image_pool(jax.random.fold_in(key_of[9], 71), 0)
    image_head = gaussian(key_of[3], (D, EMB), D ** -0.5, 0.1875)
    image_owner_keys = jax.random.split(jax.random.fold_in(key_of[4], 1), N_REPLICA * IMAGES // IMG_DEV)
    image_owner_turns = jax.random.permutation(jax.random.fold_in(key_of[4], 3), N_REPLICA * IMAGES // IMG_DEV)
    image_owner = jax.vmap(lambda own, number: deal_out(jax.random.fold_in(key_of[4], 2), own, number, IMG_DEV, N_REPLICA, 1, CAP, 2))(image_owner_keys, image_owner_turns).reshape((N_REPLICA, IMAGES, 1))
    image_slot = plant(jax.random.randint(key_of[5], (N_REPLICA, IMAGES), 0, POOL_DEV), jax.random.fold_in(key_of[5], 1), 0, POOL_DEV - 1).astype(jnp.int32)
    caption_image = plant(jax.random.randint(key_of[6], (N_REPLICA, CAPTIONS), 0, IMG_DEV), jax.random.fold_in(key_of[6], 1), 0, IMG_DEV - 1).astype(jnp.int32)
    logit_scale = jnp.clip(jax.random.uniform(key_of[7], (1,), jnp.float32, 90.0, 130.0), 90.0, 130.0)
    logit_bias = jnp.clip(jax.random.uniform(key_of[8], (1,), jnp.float32, -14.0, -10.0), -14.0, -10.0)
    return {"caption_feats": caption_feats, "text_head": text_head, "image_pool": image_pool, "image_head": image_head, "image_owner": image_owner, "image_slot": image_slot, "caption_image": caption_image, "logit_scale": logit_scale, "logit_bias": logit_bias}


def project_rows(features, head_matrix):
    projected = jnp.dot(features, head_matrix, preferred_element_type=jnp.float32)
    norm_rows = jnp.sqrt(lax.optimization_barrier(jnp.sum(projected * projected, axis=-1, keepdims=True)) + 1e-06)
    return (projected / norm_rows, norm_rows)

def pull_back(unit_rows, norm_rows, gradient):
    radial = lax.optimization_barrier(jnp.sum(unit_rows * gradient, axis=-1, keepdims=True))
    return ((gradient - unit_rows * radial) / norm_rows).astype(jnp.bfloat16)

def reference(caption_feats, text_head, image_pool, image_head, image_owner, image_slot, caption_image, logit_scale, logit_bias):
    temper = logit_scale[0]
    offset = logit_bias[0]
    column_of = jnp.arange(N_CAPTION * IMG_DEV, dtype=jnp.int32) // IMG_DEV
    block_of = jnp.arange(N_CAPTION * TXT_DEV, dtype=jnp.int32) // TXT_DEV

    def one_group(sums_now, group_args):
        pool_sum, text_sum, image_sum = sums_now
        captions, owners, slots, targets = group_args
        pool_index = (owners[:, 0] * POOL_DEV + slots).astype(jnp.int32)
        image_feats = image_pool[column_of, pool_index]
        text_unit, text_norm = project_rows(captions, text_head)
        image_unit, image_norm = project_rows(image_feats, image_head)
        text_emb = text_unit.astype(jnp.bfloat16)
        image_emb = image_unit.astype(jnp.bfloat16)
        logits = jnp.dot(text_emb, image_emb.T, preferred_element_type=jnp.float32) * temper + offset
        weights = jax.nn.sigmoid(logits).astype(jnp.bfloat16)
        positive = (block_of * IMG_DEV + targets).astype(jnp.int32)
        text_grad = temper * (jnp.dot(weights, image_emb, preferred_element_type=jnp.float32) - image_emb[positive].astype(jnp.float32))
        matched = jax.ops.segment_sum(text_emb.astype(jnp.float32), positive, num_segments=N_CAPTION * IMG_DEV)
        image_grad = temper * (jnp.dot(weights.T, text_emb, preferred_element_type=jnp.float32) - matched)
        text_proj_grad = pull_back(text_unit, text_norm, text_grad)
        image_proj_grad = pull_back(image_unit, image_norm, image_grad)
        text_feat = jnp.dot(text_proj_grad, text_head.T, preferred_element_type=jnp.float32).astype(jnp.bfloat16)
        image_feat = jnp.dot(image_proj_grad, image_head.T, preferred_element_type=jnp.float32).astype(jnp.bfloat16)
        pool_sum = pool_sum.at[column_of, pool_index].add(image_feat.astype(jnp.float32))
        text_sum = text_sum + jnp.dot(captions.T, text_proj_grad, preferred_element_type=jnp.float32)
        image_sum = image_sum + jnp.dot(image_feats.T, image_proj_grad, preferred_element_type=jnp.float32)
        return ((pool_sum, text_sum, image_sum), text_feat)
    start_sums = (jnp.zeros((N_CAPTION, N_REPLICA * POOL_DEV, D), jnp.float32), jnp.zeros((D, EMB), jnp.float32), jnp.zeros((D, EMB), jnp.float32))
    final_sums, text_feat_grad = lax.scan(one_group, start_sums, (caption_feats, image_owner, image_slot, caption_image))
    pool_sum, text_sum, image_sum = final_sums
    head_grads = jnp.stack([text_sum, image_sum], axis=1).reshape(2 * D, EMB)
    return (text_feat_grad, pool_sum.astype(jnp.bfloat16), head_grads)
```

```python
import jax
import jax.numpy as jnp
from jax import lax
from jax.sharding import Mesh
from jax.sharding import PartitionSpec as P

BF = jnp.bfloat16
F32 = jnp.float32
CAP_AXES = ("ylo", "z")
REP_AXES = ("x", "yhi", "core")
SLOTS = 12


def shifted(block, axis, distance):
    size = lax.axis_size(axis)
    return lax.ppermute(block, axis, [(i, (i + distance) % size) for i in range(size)])


def gathered_along_z(block):
    half = block.shape[0] // 2
    up, down, found = block, block, [block]
    for _ in range(3):
        up, down = shifted(up, "z", 1), shifted(down, "z", -1)
        found += [up, down]
    return found + [shifted(up[:half], "z", 1), shifted(down[half:], "z", -1)]


def project_rows(features, head_matrix):
    projected = jnp.dot(features, head_matrix, preferred_element_type=F32)
    norm_rows = jnp.sqrt(jnp.sum(projected * projected, axis=-1, keepdims=True) + 1e-06)
    return projected / norm_rows, norm_rows


def pull_back(unit_rows, norm_rows, gradient):
    radial = jnp.sum(unit_rows * gradient, axis=-1, keepdims=True)
    return ((gradient - unit_rows * radial) / norm_rows).astype(BF)


def pair_sums(resident, blocks, temper, offset):
    moving = jnp.concatenate(blocks, axis=0)
    logits = (
        lax.dot_general(resident, moving, (((1,), (1,)), ((), ())), preferred_element_type=F32)
        * temper
        + offset
    )
    weights = jax.nn.sigmoid(logits).astype(BF)
    return jnp.dot(weights, moving, preferred_element_type=F32)


def per_device(
    caption_feats,
    text_head,
    image_pool,
    image_head,
    image_owner,
    image_slot,
    caption_image,
    logit_scale,
    logit_bias,
):
    temper = logit_scale[0]
    offset = logit_bias[0]
    captions = caption_feats[0]
    pool = image_pool[0]
    owners = image_owner[:, :, 0]
    targets = caption_image[0]
    groups, images = owners.shape
    width = pool.shape[1]
    rank = lax.axis_index(REP_AXES)
    core = lax.axis_index("core")

    text_unit, text_norm = project_rows(captions, text_head)
    text_emb = text_unit.astype(BF)
    pool_unit, pool_norm = project_rows(pool, image_head)
    pool_emb = pool_unit.astype(BF)

    ids = jnp.arange(images, dtype=jnp.int32)
    owned = owners == rank
    earlier = (ids[:, None] < ids[None, :]).astype(BF)
    place = jnp.dot(owned.astype(BF), earlier, preferred_element_type=F32).astype(jnp.int32)
    wanted = jnp.arange(SLOTS, dtype=jnp.int32)[None, :, None]
    slot_table = jnp.max(
        jnp.where(owned[:, None, :] & (place[:, None, :] == wanted), image_slot[:, None, :], -1),
        axis=2,
    )
    select = (
        slot_table.reshape(-1)[:, None] == jnp.arange(pool.shape[0], dtype=jnp.int32)[None, :]
    ).astype(BF)
    mine = lax.dynamic_index_in_dim(owners, rank, 0, keepdims=False)
    my_place = jnp.sum(
        ((mine[:, None] == mine[None, :]) & (ids[None, :] < ids[:, None])).astype(jnp.int32), axis=1
    )
    hit = (
        (mine * SLOTS + my_place)[:, None]
        == jnp.arange(groups * SLOTS, dtype=jnp.int32)[None, :]
    ).astype(BF)

    outgoing = jnp.dot(select, pool_emb, preferred_element_type=F32).astype(BF)
    arrived = lax.all_to_all(
        outgoing.reshape(groups, SLOTS, width), REP_AXES, 0, 0, tiled=True
    ).reshape(groups * SLOTS, width)
    image_emb = jnp.dot(hit, arrived, preferred_element_type=F32).astype(BF)

    other_text = shifted(text_emb, "ylo", 1)
    text_blocks = gathered_along_z(text_emb)
    other_image = shifted(image_emb, "ylo", 1)
    image_blocks = gathered_along_z(image_emb)

    first = core == 0
    my_kind = jnp.where(first, captions, pool)
    its_kind = shifted(jnp.where(first, pool, captions), "core", 1)
    kind_feats = jnp.stack([jnp.where(first, my_kind, its_kind), jnp.where(first, its_kind, my_kind)])
    kind_feats = lax.all_gather(kind_feats.reshape(-1, width), "x", axis=0, tiled=True)

    target_hits = (targets[None, :] == ids[:, None]).astype(BF)
    image_sums = pair_sums(
        jnp.concatenate([image_emb, other_image]), text_blocks, temper, offset
    )
    image_rest = shifted(image_sums[images:].astype(BF), "ylo", 1)
    matched = jnp.dot(target_hits, text_emb, preferred_element_type=F32)
    image_grad = temper * (image_sums[:images] + image_rest.astype(F32) - matched)

    captions_here = captions.shape[0]
    text_sums = pair_sums(jnp.concatenate([text_emb, other_text]), image_blocks, temper, offset)
    text_rest = shifted(text_sums[captions_here:].astype(BF), "ylo", 1)
    positive = lax.dot_general(
        target_hits, image_emb, (((0,), (0,)), ((), ())), preferred_element_type=F32
    )
    text_grad = temper * (text_sums[:captions_here] + text_rest.astype(F32) - positive)

    send_back = lax.dot_general(
        hit, image_grad.astype(BF), (((0,), (0,)), ((), ())), preferred_element_type=F32
    ).astype(BF)
    received = lax.all_to_all(
        send_back.reshape(groups, SLOTS, width), REP_AXES, 0, 0, tiled=True
    ).reshape(groups * SLOTS, width)
    pool_emb_grad = lax.dot_general(
        select, received, (((0,), (0,)), ((), ())), preferred_element_type=F32
    )

    text_proj_grad = pull_back(text_unit, text_norm, text_grad)
    pool_proj_grad = pull_back(pool_unit, pool_norm, pool_emb_grad)
    back = (((1,), (1,)), ((), ()))
    text_feat_grad = lax.dot_general(
        text_proj_grad, text_head, back, preferred_element_type=F32
    ).astype(BF)
    pool_grad = lax.dot_general(
        pool_proj_grad, image_head, back, preferred_element_type=F32
    ).astype(BF)

    four = lax.axis_size("x")
    strip = width // four
    by_strip = jnp.stack(
        [
            text_proj_grad.T.reshape(four, strip, -1),
            pool_proj_grad.T.reshape(four, strip, -1),
        ],
        axis=1,
    ).reshape(2 * four, strip, -1)
    strips = lax.all_to_all(by_strip, ("x", "core"), 0, 0, tiled=True)
    kind_feats = kind_feats.reshape(2 * four, -1, width)
    part = lax.dot_general(
        kind_feats, strips, (((0, 1), (0, 2)), ((), ())), preferred_element_type=F32
    ).astype(BF)
    part = part.reshape(2, 8, four, 2, 9, strip).transpose(0, 1, 3, 2, 4, 5)
    part = lax.all_to_all(
        part.reshape(32, 9 * four, strip), ("ylo", "z", "yhi"), 0, 0, tiled=True
    )
    rows = jnp.sum(part.astype(F32), axis=0).reshape(four, 9, strip)
    rows = jnp.stack([rows[:, :5], rows[:, 4:]], axis=1).reshape(2 * four, 5, strip)
    rows = lax.all_to_all(rows, ("x", "core"), 0, 0, tiled=True)
    rows = rows.reshape(four, 2, 5, strip).transpose(2, 1, 0, 3).reshape(10, width)
    head_share = jnp.where(first, rows[:9], rows[1:])
    return text_feat_grad[None], pool_grad[None], head_share


def solution(mesh):
    fine = Mesh(mesh.devices.reshape(2, 8, 4, 2, 2), CAP_AXES + REP_AXES)
    in_specs = (
        P(REP_AXES, CAP_AXES, None),
        P(),
        P(CAP_AXES, REP_AXES, None),
        P(),
        P(None, CAP_AXES, None),
        P(None, CAP_AXES),
        P(REP_AXES, CAP_AXES),
        P(),
        P(),
    )
    out_specs = (
        P(REP_AXES, CAP_AXES, None),
        P(CAP_AXES, REP_AXES, None),
        P(CAP_AXES + REP_AXES, None),
    )
    return jax.shard_map(
        per_device, mesh=fine, in_specs=in_specs, out_specs=out_specs, check_vma=False
    )
```

```python
import jax
import jax.numpy as jnp
from jax import lax
from jax.experimental import pallas as pl
from jax.experimental.pallas import tpu as pltpu
from jax.sharding import Mesh
from jax.sharding import PartitionSpec as P

BF = jnp.bfloat16
F32 = jnp.float32
CAP_AXES = ("ylo", "z")
REP_AXES = ("x", "yhi", "core")
SLOTS = 16
VMEM = pl.BlockSpec(memory_space=pltpu.VMEM)
SMEM = pl.BlockSpec(memory_space=pltpu.SMEM)


def shifted(block, axis, distance):
    size = lax.axis_size(axis)
    return lax.ppermute(block, axis, [(i, (i + distance) % size) for i in range(size)])


def gathered_along_z(block):
    half = block.shape[0] // 2
    up, down, found = block, block, [block]
    for _ in range(3):
        up, down = shifted(up, "z", 1), shifted(down, "z", -1)
        found += [up, down]
    return found + [shifted(up[:half], "z", 1), shifted(down[half:], "z", -1)]


def call(body, outs, name, specs, *args):
    shapes = [jax.ShapeDtypeStruct(shape, dtype) for shape, dtype in outs]
    return pl.pallas_call(
        body,
        out_shape=shapes,
        in_specs=specs,
        out_specs=[VMEM] * len(shapes),
        compiler_params=pltpu.CompilerParams(vmem_limit_bytes=40 * 2**20),
        name=name,
    )(*args)


def dot(a, b, left=1, right=0):
    return lax.dot_general(a, b, (((left,), (right,)), ((), ())), preferred_element_type=F32)


def iota(shape, dim):
    return lax.broadcasted_iota(jnp.int32, shape, dim)


def one_hot(condition):
    return jnp.where(condition, 1.0, 0.0).astype(BF)


def project(features, head):
    projected = dot(features, head)
    norm = jnp.sqrt(jnp.sum(projected * projected, axis=-1, keepdims=True) + 1e-06)
    return projected / norm, norm


def pull_back(unit, norm, gradient):
    radial = jnp.sum(unit * gradient, axis=-1, keepdims=True)
    return (gradient - unit * radial) / norm


def text_front(feats_ref, head_ref, unit_ref, norm_ref, emb_ref):
    unit, norm = project(feats_ref[...], head_ref[...])
    unit_ref[...] = unit
    norm_ref[...] = norm
    emb_ref[...] = unit.astype(BF)


def pool_front(
    rank_ref, feats_ref, head_ref, owners_ref, slots_ref,
    unit_ref, norm_ref, out_ref, select_ref, hit_ref, hit_t_ref,
):
    rank = rank_ref[0]
    owners = owners_ref[...]
    groups, images = owners.shape
    rows = groups * SLOTS
    unit, norm = project(feats_ref[...], head_ref[...])
    unit_ref[...] = unit
    norm_ref[...] = norm

    row, lane = iota((images, images), 0), iota((images, images), 1)
    owned = owners == rank
    place = dot(one_hot(owned), one_hot(row < lane))
    code = jnp.where(owned, place, -1.0)
    spread = one_hot(lax.div(iota((rows, groups), 0), SLOTS) == iota((rows, groups), 1))
    code_rows = dot(spread, code.astype(BF))
    slot_rows = dot(spread, slots_ref[...].astype(F32).astype(BF))
    at = lax.rem(iota((rows, images), 0), SLOTS).astype(F32)
    slot = jnp.sum(jnp.where(code_rows == at, slot_rows + 1.0, 0.0), axis=1, keepdims=True) - 1.0
    pool_rows = unit.shape[0]
    select = one_hot(slot == iota((rows, pool_rows), 1).astype(F32))
    select_ref[...] = select
    out_ref[...] = dot(select, unit.astype(BF)).astype(BF).reshape(out_ref.shape)

    mine = jnp.sum(
        jnp.where(iota((groups, images), 0) == rank, owners.astype(F32), 0.0), axis=0, keepdims=True
    )
    mine_t = jnp.sum(jnp.where(row == lane, mine, 0.0), axis=1, keepdims=True)
    same = mine == mine_t
    spot_t = mine_t * SLOTS + jnp.sum(jnp.where(same & (lane < row), 1.0, 0.0), axis=1, keepdims=True)
    spot = mine * SLOTS + jnp.sum(jnp.where(same & (row < lane), 1.0, 0.0), axis=0, keepdims=True)
    hit_ref[...] = one_hot(spot_t == iota((images, rows), 1).astype(F32))
    hit_t_ref[...] = one_hot(spot == iota((rows, images), 0).astype(F32))


def pair_sums(scale_ref, bias_ref, own_ref, other_ref, hits_ref, partners_ref, *refs):
    *block_refs, mine_ref, rest_ref = refs
    resident = jnp.concatenate([own_ref[...], other_ref[...]], axis=0)
    total = jnp.zeros(resident.shape, F32)
    for i in range(0, len(block_refs) - 1, 2):
        moving = jnp.concatenate([block_refs[i][...], block_refs[i + 1][...]], axis=0)
        logits = dot(resident, moving, 1, 1) * scale_ref[0] + bias_ref[0]
        total += dot(jax.nn.sigmoid(logits).astype(BF), moving)
    if len(block_refs) % 2:
        moving = block_refs[-1][...]
        logits = dot(resident, moving, 1, 1) * scale_ref[0] + bias_ref[0]
        total += dot(jax.nn.sigmoid(logits).astype(BF), moving)
    own_rows = own_ref.shape[0]
    mine_ref[...] = total[:own_rows] - dot(hits_ref[...], partners_ref[...])
    rest_ref[...] = total[own_rows:].astype(BF)


def image_back(scale_ref, mine_ref, rest_ref, hit_t_ref, out_ref):
    gradient = (scale_ref[0] * (mine_ref[...] + rest_ref[...].astype(F32))).astype(BF)
    out_ref[...] = dot(hit_t_ref[...], gradient).astype(BF).reshape(out_ref.shape)


def text_back(scale_ref, mine_ref, rest_ref, unit_ref, norm_ref, grad_ref):
    gradient = scale_ref[0] * (mine_ref[...] + rest_ref[...].astype(F32))
    grad_ref[...] = pull_back(unit_ref[...], norm_ref[...], gradient).astype(BF)


def pool_back(received_ref, select_ref, unit_ref, norm_ref, text_ref, grad_ref, strips_ref):
    received = received_ref[...].reshape(select_ref.shape[0], -1)
    choose = select_ref[...].astype(F32).T.astype(BF)
    gradient = pull_back(unit_ref[...], norm_ref[...], dot(choose, received))
    grad_ref[...] = gradient.astype(BF)
    columns, _, strip, rows = strips_ref.shape
    turned = text_ref[...].astype(F32).T.astype(BF)
    strips_ref[:, 0] = turned.reshape(columns, strip, rows)
    turned = gradient.T.astype(BF)
    strips_ref[:, 1] = turned.reshape(columns, strip, rows)


def head_terms(feats_ref, strips_ref, out_ref):
    sources, strip, _ = strips_ref.shape
    grads = jnp.concatenate([strips_ref[i] for i in range(sources)], axis=1)
    terms = dot(grads, feats_ref[...])
    pieces, rows, lanes = out_ref.shape
    extra = strip - lanes
    piece = terms.shape[1] // pieces
    main = terms[:lanes].T
    blank = jnp.zeros((extra, lanes - piece), F32)
    below = jnp.zeros((rows - extra - piece, lanes), F32)
    for i in range(pieces):
        left = jnp.concatenate([terms[lanes:, i * piece : (i + 1) * piece], blank], axis=1)
        block = jnp.concatenate([left, main[i * piece : (i + 1) * piece], below], axis=0)
        out_ref[i] = block.astype(BF)


def head_sums(terms_ref, out_ref):
    pieces, rows, lanes = terms_ref.shape
    total = terms_ref[0].astype(F32)
    for i in range(1, pieces):
        total += terms_ref[i].astype(F32)
    places = out_ref.shape[0] // 2
    extra = out_ref.shape[2] - lanes
    left = total[:16].T
    left = jnp.concatenate([left[:, :16], jnp.zeros((lanes, extra - 16), F32)], axis=1)
    full = jnp.concatenate([total[16:], left[: rows - 16]], axis=1)
    for i in range(places):
        out_ref[2 * i] = full[9 * i : 9 * i + 8]
        out_ref[2 * i + 1] = full[9 * i + 4 : 9 * i + 12]


def per_device(
    caption_feats,
    text_head,
    image_pool,
    image_head,
    image_owner,
    image_slot,
    caption_image,
    logit_scale,
    logit_bias,
):
    captions = caption_feats[0]
    pool = image_pool[0]
    owners = image_owner[:, :, 0]
    targets = caption_image[0]
    groups, images = owners.shape
    texts, width = captions.shape
    pool_rows = pool.shape[0]
    rank = lax.axis_index(REP_AXES)[None]
    first = lax.axis_index("core") == 0

    text_unit, text_norm, text_emb = call(
        text_front,
        [((texts, width), F32), ((texts, 1), F32), ((texts, width), BF)],
        "text_front",
        [VMEM, VMEM],
        captions,
        text_head,
    )
    pool_unit, pool_norm, outgoing, select, hit, hit_t = call(
        pool_front,
        [
            ((pool_rows, width), F32),
            ((pool_rows, 1), F32),
            ((groups, SLOTS, width), BF),
            ((groups * SLOTS, pool_rows), BF),
            ((images, groups * SLOTS), BF),
            ((groups * SLOTS, images), BF),
        ],
        "pool_front",
        [SMEM, VMEM, VMEM, VMEM, VMEM],
        rank,
        pool,
        image_head,
        owners,
        image_slot,
    )
    other_text = shifted(text_emb, "ylo", 1)
    text_blocks = gathered_along_z(text_emb)
    arrived = lax.all_to_all(outgoing, REP_AXES, 0, 0, tiled=True)
    image_emb = dot(hit, arrived.reshape(groups * SLOTS, width)).astype(BF)
    other_image = shifted(image_emb, "ylo", 1)
    image_blocks = gathered_along_z(image_emb)

    my_kind = jnp.where(first, captions, pool)
    its_kind = shifted(jnp.where(first, pool, captions), "core", 1)
    kinds = jnp.stack([jnp.where(first, my_kind, its_kind), jnp.where(first, its_kind, my_kind)])
    kinds = lax.all_gather(kinds.reshape(-1, width), ("x", "yhi"), axis=0, tiled=True)

    ids = jnp.arange(images, dtype=jnp.int32)
    hits = one_hot(targets[None, :] == ids[:, None])
    hits_t = one_hot(targets[:, None] == ids[None, :])
    image_mine, image_rest = call(
        pair_sums,
        [((images, width), F32), ((images, width), BF)],
        "image_sums",
        [SMEM, SMEM] + [VMEM] * (4 + len(text_blocks)),
        logit_scale, logit_bias, image_emb, other_image, hits, text_emb, *text_blocks,
    )
    image_rest = shifted(image_rest, "ylo", 1)
    (send_back,) = call(
        image_back,
        [((groups, SLOTS, width), BF)],
        "image_back",
        [SMEM, VMEM, VMEM, VMEM],
        logit_scale, image_mine, image_rest, hit_t,
    )
    received = lax.all_to_all(send_back, REP_AXES, 0, 0, tiled=True)

    text_mine, text_rest = call(
        pair_sums,
        [((texts, width), F32), ((texts, width), BF)],
        "text_sums",
        [SMEM, SMEM] + [VMEM] * (4 + len(image_blocks)),
        logit_scale, logit_bias, text_emb, other_text, hits_t, image_emb, *image_blocks,
    )
    text_rest = shifted(text_rest, "ylo", 1)
    (text_grad,) = call(
        text_back,
        [((texts, width), BF)],
        "text_back",
        [SMEM, VMEM, VMEM, VMEM, VMEM],
        logit_scale, text_mine, text_rest, text_unit, text_norm,
    )
    columns = groups // 2
    strip = width // columns
    pool_proj_grad, strips = call(
        pool_back,
        [((pool_rows, width), BF), ((columns, 2, strip, texts), BF)],
        "pool_back",
        [VMEM] * 5,
        received, select, pool_unit, pool_norm, text_grad,
    )
    strips = lax.all_to_all(strips.reshape(groups, strip, texts), REP_AXES, 0, 0, tiled=True)
    text_feat_grad = dot(text_grad, text_head, 1, 1).astype(BF)
    pool_grad = dot(pool_proj_grad, image_head, 1, 1).astype(BF)

    (terms,) = call(
        head_terms, [((16, 96, 128), BF)], "head_terms", [VMEM, VMEM], kinds, strips
    )
    terms = lax.all_to_all(terms, CAP_AXES, 0, 0, tiled=True)
    (rows,) = call(head_sums, [((groups, 8, 256), F32)], "head_sums", [VMEM], terms)
    rows = lax.all_to_all(rows, REP_AXES, 0, 0, tiled=True)
    rows = rows.reshape(columns, 2, 8, 256)[:, :, :5, :strip].transpose(2, 1, 0, 3)
    rows = rows.reshape(10, width)
    head_share = jnp.where(first, rows[:9], rows[1:])
    return text_feat_grad[None], pool_grad[None], head_share


def solution(mesh):
    fine = Mesh(mesh.devices.reshape(2, 8, 4, 2, 2), CAP_AXES + REP_AXES)
    in_specs = (
        P(REP_AXES, CAP_AXES, None),
        P(),
        P(CAP_AXES, REP_AXES, None),
        P(),
        P(None, CAP_AXES, None),
        P(None, CAP_AXES),
        P(REP_AXES, CAP_AXES),
        P(),
        P(),
    )
    out_specs = (
        P(REP_AXES, CAP_AXES, None),
        P(CAP_AXES, REP_AXES, None),
        P(CAP_AXES + REP_AXES, None),
    )
    return jax.shard_map(
        per_device, mesh=fine, in_specs=in_specs, out_specs=out_specs, check_vma=False
    )
```

```python
import functools

import jax
import jax.numpy as jnp
from jax import lax
from jax.experimental import pallas as pl
from jax.experimental.pallas import tpu as pltpu
from jax.sharding import Mesh
from jax.sharding import PartitionSpec as P

BF = jnp.bfloat16
F32 = jnp.float32
CAP_AXES = ("ylo", "z")
REP_AXES = ("x", "yhi", "core")
SLOTS = 16
ANY = pl.BlockSpec(memory_space=pl.ANY)
SMEM = pl.BlockSpec(memory_space=pltpu.SMEM)


def shifted(block, axis, distance):
    size = lax.axis_size(axis)
    return lax.ppermute(block, axis, [(i, (i + distance) % size) for i in range(size)])


def gathered_along_z(block):
    half = block.shape[0] // 2
    up, down, found = block, block, [block]
    for _ in range(3):
        up, down = shifted(up, "z", 1), shifted(down, "z", -1)
        found += [up, down]
    return found + [shifted(up[:half], "z", 1), shifted(down[half:], "z", -1)]


def call(body, outs, name, scalars, arrays):
    shapes = [jax.ShapeDtypeStruct(shape, dtype) for shape, dtype in outs]
    count, total = len(arrays), len(arrays) + len(outs)

    def kernel(*refs):
        head = refs[: len(scalars)]
        far = refs[len(scalars) : len(scalars) + total]
        near = refs[len(scalars) + total : -1]
        sems = refs[-1]
        copies = [
            pltpu.make_async_copy(far[i], near[i], sems.at[i])
            if i < count
            else pltpu.make_async_copy(near[i], far[i], sems.at[i])
            for i in range(total)
        ]
        for i in range(count):
            copies[i].start()
        for i in range(count):
            copies[i].wait()
        body(*head, *near)
        for i in range(count, total):
            copies[i].start()
        for i in range(count, total):
            copies[i].wait()

    everything = [(a.shape, a.dtype) for a in arrays] + list(outs)
    return pl.pallas_call(
        kernel,
        out_shape=shapes,
        in_specs=[SMEM] * len(scalars) + [ANY] * count,
        out_specs=[ANY] * len(outs),
        scratch_shapes=[pltpu.VMEM(s, d) for s, d in everything]
        + [pltpu.SemaphoreType.DMA((total,))],
        compiler_params=pltpu.CompilerParams(vmem_limit_bytes=48 * 2**20),
        name=name,
    )(*scalars, *arrays)


def dot(a, b, left=1, right=0):
    return lax.dot_general(a, b, (((left,), (right,)), ((), ())), preferred_element_type=F32)


def iota(shape, dim):
    return lax.broadcasted_iota(jnp.int32, shape, dim)


def one_hot(condition):
    return jnp.where(condition, 1.0, 0.0).astype(BF)


def project(features, head):
    projected = dot(features, head)
    norm = jnp.sqrt(jnp.sum(projected * projected, axis=-1, keepdims=True) + 1e-06)
    return projected / norm, norm


def pull_back(unit, norm, gradient):
    radial = jnp.sum(unit * gradient, axis=-1, keepdims=True)
    return (gradient - unit * radial) / norm


def text_front(feats_ref, head_ref, unit_ref, norm_ref, emb_ref):
    unit, norm = project(feats_ref[...], head_ref[...])
    unit_ref[...] = unit
    norm_ref[...] = norm
    emb_ref[...] = unit.astype(BF)


def pool_front(
    place_ref, feats_ref, head_ref, owners_ref, slots_ref, captions_ref,
    unit_ref, norm_ref, out_ref, select_ref, hit_ref, hit_t_ref, keep_ref, give_ref,
):
    rank = place_ref[0]
    owners = owners_ref[...]
    groups, images = owners.shape
    rows = groups * SLOTS
    unit, norm = project(feats_ref[...], head_ref[...])
    unit_ref[...] = unit
    norm_ref[...] = norm

    row, lane = iota((images, images), 0), iota((images, images), 1)
    owned = owners == rank
    place = dot(one_hot(owned), one_hot(row < lane))
    code = jnp.where(owned, place, -1.0)
    spread = one_hot(lax.div(iota((rows, groups), 0), SLOTS) == iota((rows, groups), 1))
    code_rows = dot(spread, code.astype(BF))
    slot_rows = dot(spread, slots_ref[...].astype(F32).astype(BF))
    at = lax.rem(iota((rows, images), 0), SLOTS).astype(F32)
    slot = jnp.sum(jnp.where(code_rows == at, slot_rows + 1.0, 0.0), axis=1, keepdims=True) - 1.0
    pool_rows = unit.shape[0]
    select = one_hot(slot == iota((rows, pool_rows), 1).astype(F32))
    select_ref[...] = select
    out_ref[...] = dot(select, unit.astype(BF)).astype(BF).reshape(out_ref.shape)

    mine = jnp.sum(
        jnp.where(iota((groups, images), 0) == rank, owners.astype(F32), 0.0), axis=0, keepdims=True
    )
    mine_t = jnp.sum(jnp.where(row == lane, mine, 0.0), axis=1, keepdims=True)
    same = mine == mine_t
    spot_t = mine_t * SLOTS + jnp.sum(jnp.where(same & (lane < row), 1.0, 0.0), axis=1, keepdims=True)
    spot = mine * SLOTS + jnp.sum(jnp.where(same & (row < lane), 1.0, 0.0), axis=0, keepdims=True)
    hit_ref[...] = one_hot(spot_t == iota((images, rows), 1).astype(F32))
    hit_t_ref[...] = one_hot(spot == iota((rows, images), 0).astype(F32))

    @pl.when(place_ref[1] == 0)
    def _():
        keep_ref[...] = captions_ref[...]
        give_ref[...] = feats_ref[...]

    @pl.when(place_ref[1] != 0)
    def _():
        keep_ref[...] = feats_ref[...]
        give_ref[...] = captions_ref[...]


def arrive(arrived_ref, hit_ref, keep_ref, given_ref, far_ref, emb_ref, four_ref):
    arrived = arrived_ref[...].reshape(hit_ref.shape[1], -1)
    emb_ref[...] = dot(hit_ref[...], arrived).astype(BF)
    rows = keep_ref.shape[0]
    four_ref[:rows] = keep_ref[...]
    four_ref[rows : 2 * rows] = given_ref[...]
    four_ref[2 * rows :] = far_ref[...]


def pair_sums(turned, scale_ref, bias_ref, own_ref, other_ref, targets_ref, partners_ref, *refs):
    *block_refs, mine_ref, rest_ref = refs
    resident = jnp.concatenate([own_ref[...], other_ref[...]], axis=0)
    total = jnp.zeros(resident.shape, F32)
    groups = [block_refs[:1]] + [block_refs[i : i + 2] for i in range(1, len(block_refs), 2)]
    for group in groups:
        moving = jnp.concatenate([ref[...] for ref in group], axis=0)
        logits = dot(resident, moving, 1, 1) * scale_ref[0] + bias_ref[0]
        total += dot(jax.nn.sigmoid(logits).astype(BF), moving)
    own_rows, partner_rows = own_ref.shape[0], partners_ref.shape[0]
    images, texts = (partner_rows, own_rows) if turned else (own_rows, partner_rows)
    hits = jnp.where(targets_ref[...] == iota((images, texts), 0), 1.0, 0.0)
    hits = hits.T if turned else hits
    mine_ref[...] = total[:own_rows] - dot(hits.astype(BF), partners_ref[...])
    rest_ref[...] = total[own_rows:].astype(BF)


def image_back(scale_ref, mine_ref, rest_ref, hit_t_ref, out_ref):
    gradient = (scale_ref[0] * (mine_ref[...] + rest_ref[...].astype(F32))).astype(BF)
    out_ref[...] = dot(hit_t_ref[...], gradient).astype(BF).reshape(out_ref.shape)


def text_back(scale_ref, mine_ref, rest_ref, unit_ref, norm_ref, grad_ref):
    gradient = scale_ref[0] * (mine_ref[...] + rest_ref[...].astype(F32))
    grad_ref[...] = pull_back(unit_ref[...], norm_ref[...], gradient).astype(BF)


def pool_back(received_ref, select_ref, unit_ref, norm_ref, text_ref, grad_ref, strips_ref):
    received = received_ref[...].reshape(select_ref.shape[0], -1)
    choose = select_ref[...].astype(F32).T.astype(BF)
    gradient = pull_back(unit_ref[...], norm_ref[...], dot(choose, received))
    grad_ref[...] = gradient.astype(BF)
    columns, _, strip, rows = strips_ref.shape
    turned = text_ref[...].astype(F32).T.astype(BF)
    strips_ref[:, 0] = turned.reshape(columns, strip, rows)
    turned = gradient.T.astype(BF)
    strips_ref[:, 1] = turned.reshape(columns, strip, rows)


def head_terms(place_ref, strips_ref, home_ref, up_ref, down_ref, far_up_ref, far_down_ref, out_ref):
    x, yhi, core = place_ref[2], place_ref[3], place_ref[1]
    _, strip, lanes = strips_ref.shape
    extra = strip - lanes

    def grads(along, across):
        blocks = []
        for dy in across:
            for dc in range(2):
                source = lax.rem(x + along, 4) * 4 + lax.rem(yhi + dy, 2) * 2 + lax.rem(core + dc, 2)
                blocks.append(strips_ref[source])
        block = jnp.concatenate(blocks, axis=1)
        return jnp.concatenate([block[:lanes]] + [block[lanes:]] * (lanes // extra), axis=0)

    terms = dot(grads(0, (0, 1)), home_ref[...])
    terms += dot(grads(3, (0, 1)), up_ref[...])
    terms += dot(grads(1, (0, 1)), down_ref[...])
    terms += dot(grads(2, (0,)), far_up_ref[...])
    terms += dot(grads(2, (1,)), far_down_ref[...])
    turned = terms.T
    turned = jnp.concatenate([turned, jnp.zeros((8, 2 * lanes), F32)], axis=0)
    row, lane = iota((8, lanes), 0), iota((8, lanes), 1)
    diagonal = (lax.div(lane, extra) == row) & (row < 5)
    for pair in range(out_ref.shape[0]):
        halves = []
        for start in (9 * pair, 9 * pair + 4):
            last = jnp.where(diagonal, turned[start : start + 8, lanes:], 0.0)
            last = jnp.sum(last, axis=0, keepdims=True)
            main = turned[start : start + 8, :lanes]
            halves.append(jnp.where(row < 5, main, jnp.where(row == 5, last, 0.0)))
        out_ref[pair] = jnp.concatenate(halves, axis=0).astype(BF)


def head_sums(place_ref, terms_ref, out_ref):
    core = place_ref[1]
    lanes = terms_ref.shape[2]
    extra = out_ref.shape[1] // 8 - lanes
    row, lane = iota((16, lanes), 0), iota((16, lanes), 1)
    diagonal = lax.div(lane, extra) == lax.rem(row, 8)
    fold = jnp.where(lax.rem(iota((lanes, extra), 0), extra) == iota((lanes, extra), 1), 1.0, 0.0)
    strips = []
    for k in range(8):
        total = terms_ref[k].astype(F32)
        for i in range(1, 16):
            total += terms_ref[8 * i + k].astype(F32)
        last = jnp.where(row < 8, total[5:6], total[13:14])
        last = jnp.where(diagonal, last, 0.0)
        last = jnp.dot(last, fold, preferred_element_type=F32, precision=lax.Precision.HIGHEST)
        strips += [total, last]
    rows = jnp.concatenate(strips, axis=1)
    to, source = iota((16, 16), 0), iota((16, 16), 1)
    order = jnp.where(2 * lax.rem(source, 8) + lax.div(source, 8) == to + core, 1.0, 0.0)
    rows = jnp.dot(order, rows, preferred_element_type=F32, precision=lax.Precision.HIGHEST)
    out_ref[...] = rows[: out_ref.shape[0]]


def per_device(
    caption_feats,
    text_head,
    image_pool,
    image_head,
    image_owner,
    image_slot,
    caption_image,
    logit_scale,
    logit_bias,
):
    captions = caption_feats[0]
    pool = image_pool[0]
    owners = image_owner[:, :, 0]
    groups, images = owners.shape
    texts, width = captions.shape
    pool_rows = pool.shape[0]
    place = jnp.stack([lax.axis_index(REP_AXES)] + [lax.axis_index(a) for a in ("core", "x", "yhi")])

    text_unit, text_norm, text_emb = call(
        text_front,
        [((texts, width), F32), ((texts, 1), F32), ((texts, width), BF)],
        "text_front", [], [captions, text_head],
    )
    pool_unit, pool_norm, outgoing, select, hit, hit_t, keep, give = call(
        pool_front,
        [
            ((pool_rows, width), F32),
            ((pool_rows, 1), F32),
            ((groups, SLOTS, width), BF),
            ((groups * SLOTS, pool_rows), BF),
            ((images, groups * SLOTS), BF),
            ((groups * SLOTS, images), BF),
            ((texts, width), BF),
            ((texts, width), BF),
        ],
        "pool_front", [place], [pool, image_head, owners, image_slot, captions],
    )
    other_text = shifted(text_emb, "ylo", 1)
    text_blocks = gathered_along_z(text_emb)
    arrived = lax.all_to_all(outgoing, REP_AXES, 0, 0, tiled=True)
    given = shifted(give, "core", 1)
    far = shifted(jnp.concatenate([keep, given]), "yhi", 1)
    image_emb, four = call(
        arrive, [((images, width), BF), ((4 * texts, width), BF)], "arrive", [],
        [arrived, hit, keep, given, far],
    )
    other_image = shifted(image_emb, "ylo", 1)
    image_blocks = gathered_along_z(image_emb)
    up, down = shifted(four, "x", 1), shifted(four, "x", -1)
    far_up, far_down = shifted(up[: 2 * texts], "x", 1), shifted(down[2 * texts :], "x", -1)

    scalars = [logit_scale, logit_bias]
    image_mine, image_rest = call(
        functools.partial(pair_sums, False),
        [((images, width), F32), ((images, width), BF)],
        "image_sums", scalars, [image_emb, other_image, caption_image, text_emb, *text_blocks],
    )
    image_rest = shifted(image_rest, "ylo", 1)
    (send_back,) = call(
        image_back, [((groups, SLOTS, width), BF)], "image_back", scalars[:1],
        [image_mine, image_rest, hit_t],
    )
    received = lax.all_to_all(send_back, REP_AXES, 0, 0, tiled=True)

    text_mine, text_rest = call(
        functools.partial(pair_sums, True),
        [((texts, width), F32), ((texts, width), BF)],
        "text_sums", scalars, [text_emb, other_text, caption_image, image_emb, *image_blocks],
    )
    text_rest = shifted(text_rest, "ylo", 1)
    (text_grad,) = call(
        text_back, [((texts, width), BF)], "text_back", scalars[:1],
        [text_mine, text_rest, text_unit, text_norm],
    )
    columns = groups // 2
    strip = width // columns
    pool_proj_grad, strips = call(
        pool_back,
        [((pool_rows, width), BF), ((columns, 2, strip, texts), BF)],
        "pool_back", [], [received, select, pool_unit, pool_norm, text_grad],
    )
    strips = lax.all_to_all(strips.reshape(groups, strip, texts), REP_AXES, 0, 0, tiled=True)
    text_feat_grad = dot(text_grad, text_head, 1, 1).astype(BF)
    pool_grad = dot(pool_proj_grad, image_head, 1, 1).astype(BF)

    (terms,) = call(
        head_terms, [((128, 16, 128), BF)], "head_terms", [place],
        [strips, four, up, down, far_up, far_down],
    )
    terms = lax.all_to_all(terms.reshape(256, 8, 128), CAP_AXES + REP_AXES, 0, 0, tiled=True)
    (head_share,) = call(
        head_sums, [((9, width), F32)], "head_sums", [place], [terms.reshape(128, 16, 128)]
    )
    return text_feat_grad[None], pool_grad[None], head_share


def solution(mesh):
    fine = Mesh(mesh.devices.reshape(2, 8, 4, 2, 2), CAP_AXES + REP_AXES)
    in_specs = (
        P(REP_AXES, CAP_AXES, None),
        P(),
        P(CAP_AXES, REP_AXES, None),
        P(),
        P(None, CAP_AXES, None),
        P(None, CAP_AXES),
        P(REP_AXES, CAP_AXES),
        P(),
        P(),
    )
    out_specs = (
        P(REP_AXES, CAP_AXES, None),
        P(CAP_AXES, REP_AXES, None),
        P(CAP_AXES + REP_AXES, None),
    )
    return jax.shard_map(
        per_device, mesh=fine, in_specs=in_specs, out_specs=out_specs, check_vma=False
    )
```

```python
import functools

import jax
import jax.numpy as jnp
from jax import lax
from jax.experimental import pallas as pl
from jax.experimental.pallas import tpu as pltpu
from jax.sharding import Mesh
from jax.sharding import PartitionSpec as P

BF = jnp.bfloat16
F32 = jnp.float32
CAP_AXES = ("ylo", "z")
REP_AXES = ("x", "yhi", "core")
SLOTS = 16
FAR = pl.BlockSpec(memory_space=pltpu.HBM)
SMEM = pl.BlockSpec(memory_space=pltpu.SMEM)


def shifted(block, axis, distance):
    size = lax.axis_size(axis)
    return lax.ppermute(block, axis, [(i, (i + distance) % size) for i in range(size)])


def gathered_along_z(block, way):
    ahead, behind, found = block, block, [block]
    for _ in range(3):
        ahead, behind = shifted(ahead, "z", way), shifted(behind, "z", -way)
        found += [ahead, behind]
    return found + [shifted(ahead, "z", way)]


def call(body, outs, name, scalars, arrays):
    shapes = [jax.ShapeDtypeStruct(shape, dtype) for shape, dtype in outs]
    count, total = len(arrays), len(arrays) + len(outs)

    def kernel(*refs):
        head = refs[: len(scalars)]
        far = refs[len(scalars) : len(scalars) + total]
        near = refs[len(scalars) + total : -1]
        sems = refs[-1]
        copies = [
            pltpu.make_async_copy(far[i], near[i], sems.at[i])
            if i < count
            else pltpu.make_async_copy(near[i], far[i], sems.at[i])
            for i in range(total)
        ]
        for i in range(count):
            copies[i].start()
        for i in range(count):
            copies[i].wait()
        body(*head, *near)
        for i in range(count, total):
            copies[i].start()
        for i in range(count, total):
            copies[i].wait()

    everything = [(a.shape, a.dtype) for a in arrays] + list(outs)
    return pl.pallas_call(
        kernel,
        out_shape=shapes,
        in_specs=[SMEM] * len(scalars) + [FAR] * count,
        out_specs=[FAR] * len(outs),
        scratch_shapes=[pltpu.VMEM(s, d) for s, d in everything]
        + [pltpu.SemaphoreType.DMA((total,))],
        compiler_params=pltpu.CompilerParams(vmem_limit_bytes=64 * 2**20),
        name=name,
    )(*scalars, *arrays)


def dot(a, b, left=1, right=0):
    return lax.dot_general(a, b, (((left,), (right,)), ((), ())), preferred_element_type=F32)


def iota(shape, dim):
    return lax.broadcasted_iota(jnp.int32, shape, dim)


def one_hot(condition):
    return jnp.where(condition, 1.0, 0.0).astype(BF)


def project(features, head):
    projected = dot(features, head)
    norm = jnp.sqrt(jnp.sum(projected * projected, axis=-1, keepdims=True) + 1e-06)
    return projected / norm, norm


def pull_back(unit, norm, gradient):
    radial = jnp.sum(unit * gradient, axis=-1, keepdims=True)
    return (gradient - unit * radial) / norm


def text_front(feats_ref, head_ref, after_ref, unit_ref, norm_ref, emb_ref):
    unit, norm = project(feats_ref[...], head_ref[...])
    unit_ref[...] = unit
    norm_ref[...] = norm
    emb_ref[...] = unit.astype(BF)


def pool_front(
    place_ref, feats_ref, head_ref, owners_ref, slots_ref, unit_ref, norm_ref, out_ref, select_ref
):
    rank = place_ref[0]
    owners = owners_ref[...]
    groups, images = owners.shape
    rows = groups * SLOTS
    unit, norm = project(feats_ref[...], head_ref[...])
    unit_ref[...] = unit
    norm_ref[...] = norm

    row, lane = iota((images, images), 0), iota((images, images), 1)
    owned = owners == rank
    place = dot(one_hot(owned), one_hot(row < lane))
    code = jnp.where(owned, place, -1.0)
    spread = one_hot(lax.div(iota((rows, groups), 0), SLOTS) == iota((rows, groups), 1))
    code_rows = dot(spread, code.astype(BF))
    slot_rows = dot(spread, slots_ref[...].astype(F32).astype(BF))
    at = lax.rem(iota((rows, images), 0), SLOTS).astype(F32)
    slot = jnp.sum(jnp.where(code_rows == at, slot_rows + 1.0, 0.0), axis=1, keepdims=True) - 1.0
    pool_rows = unit.shape[0]
    select = one_hot(slot == iota((rows, pool_rows), 1).astype(F32))
    select_ref[...] = select
    out_ref[...] = dot(select, unit.astype(BF)).astype(BF).reshape(out_ref.shape)


def requested(place_ref, owners_ref, turned):
    owners = owners_ref[...]
    groups, images = owners.shape
    row, lane = iota((images, images), 0), iota((images, images), 1)
    mine = jnp.sum(
        jnp.where(iota((groups, images), 0) == place_ref[0], owners.astype(F32), 0.0),
        axis=0,
        keepdims=True,
    )
    mine_t = jnp.sum(jnp.where(row == lane, mine, 0.0), axis=1, keepdims=True)
    same = mine == mine_t
    if turned:
        before = jnp.sum(jnp.where(same & (row < lane), 1.0, 0.0), axis=0, keepdims=True)
        rows = iota((groups * SLOTS, images), 0)
        return one_hot(mine * SLOTS + before == rows.astype(F32))
    before = jnp.sum(jnp.where(same & (lane < row), 1.0, 0.0), axis=1, keepdims=True)
    return one_hot(mine_t * SLOTS + before == iota((images, groups * SLOTS), 1).astype(F32))


def arrive(place_ref, arrived_ref, owners_ref, captions_ref, pool_ref, emb_ref, keep_ref, give_ref):
    hit = requested(place_ref, owners_ref, False)
    emb_ref[...] = dot(hit, arrived_ref[...].reshape(hit.shape[1], -1)).astype(BF)

    @pl.when(place_ref[1] == 0)
    def _():
        keep_ref[...] = captions_ref[...]
        give_ref[...] = pool_ref[...]

    @pl.when(place_ref[1] != 0)
    def _():
        keep_ref[...] = pool_ref[...]
        give_ref[...] = captions_ref[...]


def joined(a_ref, b_ref, c_ref, d_ref, ab_ref, cd_ref):
    rows = a_ref.shape[0]
    ab_ref[:rows] = a_ref[...]
    ab_ref[rows:] = b_ref[...]
    cd_ref[:rows] = c_ref[...]
    cd_ref[rows:] = d_ref[...]


def pair_sums(turned, scale_ref, bias_ref, own_ref, other_ref, targets_ref, partners_ref, *refs):
    *block_refs, mine_ref, rest_ref = refs
    resident = jnp.concatenate([own_ref[...], other_ref[...]], axis=0)
    total = jnp.zeros(resident.shape, F32)
    groups = [block_refs[:1]] + [block_refs[i : i + 2] for i in range(1, len(block_refs), 2)]
    for group in groups:
        moving = jnp.concatenate([ref[...] for ref in group], axis=0)
        logits = dot(resident, moving, 1, 1) * scale_ref[0] + bias_ref[0]
        total += dot(jax.nn.sigmoid(logits).astype(BF), moving)
    own_rows, partner_rows = own_ref.shape[0], partners_ref.shape[0]
    images, texts = (partner_rows, own_rows) if turned else (own_rows, partner_rows)
    hits = jnp.where(targets_ref[...] == iota((images, texts), 0), 1.0, 0.0)
    hits = hits.T if turned else hits
    mine_ref[...] = total[:own_rows] - dot(hits.astype(BF), partners_ref[...])
    rest_ref[...] = total[own_rows:].astype(BF)


def image_back(place_ref, scale_ref, mine_ref, rest_ref, owners_ref, out_ref):
    gradient = (scale_ref[0] * (mine_ref[...] + rest_ref[...].astype(F32))).astype(BF)
    out_ref[...] = dot(requested(place_ref, owners_ref, True), gradient).astype(BF).reshape(out_ref.shape)


def text_back(scale_ref, mine_ref, rest_ref, unit_ref, norm_ref, grad_ref):
    gradient = scale_ref[0] * (mine_ref[...] + rest_ref[...].astype(F32))
    grad_ref[...] = pull_back(unit_ref[...], norm_ref[...], gradient).astype(BF)


def pool_back(received_ref, select_ref, unit_ref, norm_ref, text_ref, grad_ref, strips_ref):
    received = received_ref[...].reshape(select_ref.shape[0], -1)
    choose = select_ref[...].astype(F32).T.astype(BF)
    gradient = pull_back(unit_ref[...], norm_ref[...], dot(choose, received))
    grad_ref[...] = gradient.astype(BF)
    columns, _, strip, rows = strips_ref.shape
    turned = text_ref[...].astype(F32).T.astype(BF)
    strips_ref[:, 0] = turned.reshape(columns, strip, rows)
    turned = gradient.T.astype(BF)
    strips_ref[:, 1] = turned.reshape(columns, strip, rows)


def head_terms(place_ref, strips_ref, *refs):
    x, yhi, core = place_ref[2], place_ref[3], place_ref[1]
    *feats_refs, out_ref = refs
    _, strip, lanes = strips_ref.shape
    extra = strip - lanes
    terms = jnp.zeros((2 * lanes, feats_refs[0].shape[1]), F32)
    for i, feats_ref in enumerate(feats_refs):
        along, across = (0, 3, 1, 2)[i // 2], i % 2
        blocks = []
        for dc in range(2):
            source = lax.rem(x + along, 4) * 4 + lax.rem(yhi + across, 2) * 2 + lax.rem(core + dc, 2)
            blocks.append(strips_ref[source])
        block = jnp.concatenate(blocks, axis=1)
        block = jnp.concatenate([block[:lanes]] + [block[lanes:]] * (lanes // extra), axis=0)
        terms += dot(block, feats_ref[...])
    turned = terms.T
    turned = jnp.concatenate([turned, jnp.zeros((8, 2 * lanes), F32)], axis=0)
    row, lane = iota((8, lanes), 0), iota((8, lanes), 1)
    diagonal = (lax.div(lane, extra) == row) & (row < 5)
    for pair in range(out_ref.shape[0]):
        halves = []
        for start in (9 * pair, 9 * pair + 4):
            last = jnp.where(diagonal, turned[start : start + 8, lanes:], 0.0)
            last = jnp.sum(last, axis=0, keepdims=True)
            main = turned[start : start + 8, :lanes]
            halves.append(jnp.where(row < 5, main, jnp.where(row == 5, last, 0.0)))
        out_ref[pair] = jnp.concatenate(halves, axis=0).astype(BF)


def head_sums(place_ref, terms_ref, out_ref):
    core = place_ref[1]
    lanes = terms_ref.shape[2]
    extra = out_ref.shape[1] // 8 - lanes
    row, lane = iota((16, lanes), 0), iota((16, lanes), 1)
    diagonal = lax.div(lane, extra) == lax.rem(row, 8)
    fold = jnp.where(lax.rem(iota((lanes, extra), 0), extra) == iota((lanes, extra), 1), 1.0, 0.0)
    strips = []
    for k in range(8):
        total = terms_ref[k].astype(F32)
        for i in range(1, 16):
            total += terms_ref[8 * i + k].astype(F32)
        last = jnp.where(row < 8, total[5:6], total[13:14])
        last = jnp.where(diagonal, last, 0.0)
        last = jnp.dot(last, fold, preferred_element_type=F32, precision=lax.Precision.HIGHEST)
        strips += [total, last]
    rows = jnp.concatenate(strips, axis=1)
    to, source = iota((16, 16), 0), iota((16, 16), 1)
    order = jnp.where(2 * lax.rem(source, 8) + lax.div(source, 8) == to + core, 1.0, 0.0)
    rows = jnp.dot(order, rows, preferred_element_type=F32, precision=lax.Precision.HIGHEST)
    out_ref[...] = rows[: out_ref.shape[0]]


def per_device(
    caption_feats,
    text_head,
    image_pool,
    image_head,
    image_owner,
    image_slot,
    caption_image,
    logit_scale,
    logit_bias,
):
    captions = caption_feats[0]
    pool = image_pool[0]
    owners = image_owner[:, :, 0]
    groups, images = owners.shape
    texts, width = captions.shape
    pool_rows = pool.shape[0]
    place = jnp.stack([lax.axis_index(REP_AXES)] + [lax.axis_index(a) for a in ("core", "x", "yhi")])

    pool_unit, pool_norm, outgoing, select = call(
        pool_front,
        [
            ((pool_rows, width), F32),
            ((pool_rows, 1), F32),
            ((groups, SLOTS, width), BF),
            ((groups * SLOTS, pool_rows), BF),
        ],
        "pool_front", [place], [pool, image_head, owners, image_slot],
    )
    arrived = lax.all_to_all(outgoing, REP_AXES, 0, 0, tiled=True)
    text_unit, text_norm, text_emb = call(
        text_front,
        [((texts, width), F32), ((texts, 1), F32), ((texts, width), BF)],
        "text_front", [], [captions, text_head, pool_norm],
    )
    other_text = shifted(text_emb, "ylo", 1)
    text_blocks = gathered_along_z(text_emb, 1)
    image_emb, keep, give = call(
        arrive, [((images, width), BF), ((texts, width), BF), ((texts, width), BF)],
        "arrive", [place], [arrived, owners, captions, pool],
    )
    other_image = shifted(image_emb, "ylo", 1)
    image_blocks = gathered_along_z(image_emb, -1)

    given = shifted(give, "core", 1)
    far_keep = shifted(keep, "yhi", 1)
    far_given = lax.ppermute(give, ("yhi", "core"), [(i, 3 - i) for i in range(4)])
    home, far = call(
        joined, [((2 * texts, width), BF)] * 2, "joined", [], [keep, given, far_keep, far_given]
    )
    feats = [home, far]
    feats += [shifted(home, "x", 1), shifted(far, "x", 1)]
    feats += [shifted(home, "x", -1), shifted(far, "x", -1)]
    feats += [shifted(feats[2], "x", 1), shifted(feats[5], "x", -1)]

    scalars = [logit_scale, logit_bias]
    image_mine, image_rest = call(
        functools.partial(pair_sums, False),
        [((images, width), F32), ((images, width), BF)],
        "image_sums", scalars, [image_emb, other_image, caption_image, text_emb, *text_blocks],
    )
    image_rest = shifted(image_rest, "ylo", 1)
    (send_back,) = call(
        image_back, [((groups, SLOTS, width), BF)], "image_back",
        [place, logit_scale], [image_mine, image_rest, owners],
    )
    received = lax.all_to_all(send_back, REP_AXES, 0, 0, tiled=True)

    text_mine, text_rest = call(
        functools.partial(pair_sums, True),
        [((texts, width), F32), ((texts, width), BF)],
        "text_sums", scalars, [text_emb, other_text, caption_image, image_emb, *image_blocks],
    )
    text_rest = shifted(text_rest, "ylo", 1)
    (text_grad,) = call(
        text_back, [((texts, width), BF)], "text_back", scalars[:1],
        [text_mine, text_rest, text_unit, text_norm],
    )
    columns = groups // 2
    strip = width // columns
    pool_proj_grad, strips = call(
        pool_back,
        [((pool_rows, width), BF), ((columns, 2, strip, texts), BF)],
        "pool_back", [], [received, select, pool_unit, pool_norm, text_grad],
    )
    strips = lax.all_to_all(strips.reshape(groups, strip, texts), REP_AXES, 0, 0, tiled=True)
    text_feat_grad = dot(text_grad, text_head, 1, 1).astype(BF)
    pool_grad = dot(pool_proj_grad, image_head, 1, 1).astype(BF)

    (terms,) = call(
        head_terms, [((128, 16, 128), BF)], "head_terms", [place],
        [strips, *feats],
    )
    terms = lax.all_to_all(terms.reshape(256, 8, 128), CAP_AXES + REP_AXES, 0, 0, tiled=True)
    (head_share,) = call(
        head_sums, [((9, width), F32)], "head_sums", [place], [terms.reshape(128, 16, 128)]
    )
    return text_feat_grad[None], pool_grad[None], head_share


def solution(mesh):
    fine = Mesh(mesh.devices.reshape(2, 8, 4, 2, 2), CAP_AXES + REP_AXES)
    in_specs = (
        P(REP_AXES, CAP_AXES, None),
        P(),
        P(CAP_AXES, REP_AXES, None),
        P(),
        P(None, CAP_AXES, None),
        P(None, CAP_AXES),
        P(REP_AXES, CAP_AXES),
        P(),
        P(),
    )
    out_specs = (
        P(REP_AXES, CAP_AXES, None),
        P(CAP_AXES, REP_AXES, None),
        P(CAP_AXES + REP_AXES, None),
    )
    return jax.shard_map(
        per_device, mesh=fine, in_specs=in_specs, out_specs=out_specs, check_vma=False
    )
```

```python
import functools

import jax
import jax.numpy as jnp
from jax import lax
from jax.experimental import pallas as pl
from jax.experimental.pallas import tpu as pltpu
from jax.sharding import Mesh
from jax.sharding import PartitionSpec as P

BF = jnp.bfloat16
F32 = jnp.float32
CAP_AXES = ("ylo", "z")
REP_AXES = ("x", "yhi", "core")
SLOTS = 16
FAR = pl.BlockSpec(memory_space=pltpu.HBM)
SMEM = pl.BlockSpec(memory_space=pltpu.SMEM)


def shifted(block, axis, distance):
    size = lax.axis_size(axis)
    return lax.ppermute(block, axis, [(i, (i + distance) % size) for i in range(size)])


def gathered_along_z(block, way):
    ahead, behind, found = block, block, [block]
    for _ in range(3):
        ahead, behind = shifted(ahead, "z", way), shifted(behind, "z", -way)
        found += [ahead, behind]
    return found + [shifted(ahead, "z", way)]


def call(body, outs, name, scalars, arrays, after=()):
    shapes = [jax.ShapeDtypeStruct(shape, dtype) for shape, dtype in outs]
    count, total = len(arrays), len(arrays) + len(outs)

    def kernel(*refs):
        head = refs[: len(scalars)]
        far = refs[len(scalars) :][:count] + refs[len(scalars) + count + len(after) :][: len(outs)]
        near = refs[len(scalars) + len(after) + total : -1]
        sems = refs[-1]
        copies = [
            pltpu.make_async_copy(far[i], near[i], sems.at[i])
            if i < count
            else pltpu.make_async_copy(near[i], far[i], sems.at[i])
            for i in range(total)
        ]
        for i in range(count):
            copies[i].start()
        for i in range(count):
            copies[i].wait()
        body(*head, *near)
        for i in range(count, total):
            copies[i].start()
        for i in range(count, total):
            copies[i].wait()

    everything = [(a.shape, a.dtype) for a in arrays] + list(outs)
    return pl.pallas_call(
        kernel,
        out_shape=shapes,
        in_specs=[SMEM] * len(scalars) + [FAR] * (count + len(after)),
        out_specs=[FAR] * len(outs),
        scratch_shapes=[pltpu.VMEM(s, d) for s, d in everything]
        + [pltpu.SemaphoreType.DMA((total,))],
        compiler_params=pltpu.CompilerParams(vmem_limit_bytes=64 * 2**20),
        name=name,
    )(*scalars, *arrays, *after)


def dot(a, b, left=1, right=0):
    return lax.dot_general(a, b, (((left,), (right,)), ((), ())), preferred_element_type=F32)


def iota(shape, dim):
    return lax.broadcasted_iota(jnp.int32, shape, dim)


def one_hot(condition):
    return jnp.where(condition, 1.0, 0.0).astype(BF)


def pull_back(unit, norm, gradient):
    radial = jnp.sum(unit * gradient, axis=-1, keepdims=True)
    return (gradient - unit * radial) / norm


def front(
    place_ref, owners_far, slots_far, pool_far, image_head_far, captions_far, text_head_far,
    pool_unit_far, pool_norm_far, out_far, select_far, text_unit_far, text_norm_far, emb_far,
    owners_ref, slots_ref, pool_ref, image_head_ref, captions_ref, text_head_ref,
    pool_unit_ref, pool_norm_ref, out_ref, select_ref, text_unit_ref, text_norm_ref, emb_ref, sems,
):
    width = pool_ref.shape[1]
    depth = width // 3
    used = [0]

    def moved(source, target):
        copy = pltpu.make_async_copy(source, target, sems.at[used[0]])
        used[0] += 1
        copy.start()
        return copy

    def cut(far, ref):
        rows = [pl.ds(i * depth, depth) for i in range(3)]
        return [moved(far.at[r], ref.at[r]) for r in rows]

    small = [moved(owners_far, owners_ref), moved(slots_far, slots_ref)]
    pool_in = moved(pool_far, pool_ref)
    image_head_in = cut(image_head_far, image_head_ref)
    captions_in = moved(captions_far, captions_ref)
    text_head_in = cut(text_head_far, text_head_ref)

    def projected(feats_ref, head_ref, head_in):
        total = jnp.zeros((feats_ref.shape[0], width), F32)
        for i in range(3):
            head_in[i].wait()
            rows = pl.ds(i * depth, depth)
            total += dot(feats_ref[:, rows], head_ref[rows])
        norm = jnp.sqrt(jnp.sum(total * total, axis=-1, keepdims=True) + 1e-06)
        return total / norm, norm

    for copy in small:
        copy.wait()
    owners = owners_ref[...]
    groups, images = owners.shape
    rows = groups * SLOTS
    owned = owners == place_ref[0]
    place = dot(one_hot(owned), one_hot(iota((images, images), 0) < iota((images, images), 1)))
    code = jnp.where(owned, place, -1.0)
    spread = one_hot(lax.div(iota((rows, groups), 0), SLOTS) == iota((rows, groups), 1))
    code_rows = dot(spread, code.astype(BF))
    slot_rows = dot(spread, slots_ref[...].astype(F32).astype(BF))
    at = lax.rem(iota((rows, images), 0), SLOTS).astype(F32)
    slot = jnp.sum(jnp.where(code_rows == at, slot_rows + 1.0, 0.0), axis=1, keepdims=True) - 1.0
    select = one_hot(slot == iota((rows, pool_ref.shape[0]), 1).astype(F32))
    select_ref[...] = select
    outs = [moved(select_ref, select_far)]

    pool_in.wait()
    unit, norm = projected(pool_ref, image_head_ref, image_head_in)
    pool_unit_ref[...] = unit
    pool_norm_ref[...] = norm
    out_ref[...] = dot(select, unit.astype(BF)).astype(BF).reshape(out_ref.shape)
    outs += [
        moved(out_ref, out_far),
        moved(pool_unit_ref, pool_unit_far),
        moved(pool_norm_ref, pool_norm_far),
    ]

    captions_in.wait()
    unit, norm = projected(captions_ref, text_head_ref, text_head_in)
    emb_ref[...] = unit.astype(BF)
    outs += [moved(emb_ref, emb_far)]
    text_unit_ref[...] = unit
    text_norm_ref[...] = norm
    outs += [moved(text_unit_ref, text_unit_far), moved(text_norm_ref, text_norm_far)]
    for copy in outs:
        copy.wait()


def requested(place_ref, owners_ref, turned):
    owners = owners_ref[...]
    groups, images = owners.shape
    row, lane = iota((images, images), 0), iota((images, images), 1)
    mine = jnp.sum(
        jnp.where(iota((groups, images), 0) == place_ref[0], owners.astype(F32), 0.0),
        axis=0,
        keepdims=True,
    )
    mine_t = jnp.sum(jnp.where(row == lane, mine, 0.0), axis=1, keepdims=True)
    same = mine == mine_t
    if turned:
        before = jnp.sum(jnp.where(same & (row < lane), 1.0, 0.0), axis=0, keepdims=True)
        rows = iota((groups * SLOTS, images), 0)
        return one_hot(mine * SLOTS + before == rows.astype(F32))
    before = jnp.sum(jnp.where(same & (lane < row), 1.0, 0.0), axis=1, keepdims=True)
    return one_hot(mine_t * SLOTS + before == iota((images, groups * SLOTS), 1).astype(F32))


def sorted_kinds(place_ref, captions_ref, pool_ref, keep_ref, give_ref):
    first = place_ref[1] == 0
    keep_ref[...] = jnp.where(first, captions_ref[...], pool_ref[...])
    give_ref[...] = jnp.where(first, pool_ref[...], captions_ref[...])


def arrive(place_ref, arrived_ref, owners_ref, emb_ref):
    hit = requested(place_ref, owners_ref, False)
    emb_ref[...] = dot(hit, arrived_ref[...].reshape(hit.shape[1], -1)).astype(BF)


def joined(a_ref, b_ref, c_ref, d_ref, out_ref):
    rows = a_ref.shape[0]
    for i, ref in enumerate((a_ref, b_ref, c_ref, d_ref)):
        out_ref[i * rows : (i + 1) * rows] = ref[...]


def pair_sums(turned, scale_ref, bias_ref, own_ref, other_ref, targets_ref, partners_ref, *refs):
    *block_refs, mine_ref, rest_ref = refs
    resident = jnp.concatenate([own_ref[...], other_ref[...]], axis=0)
    total = jnp.zeros(resident.shape, F32)
    if len(block_refs) == 1:
        groups = [[block_refs[0].at[pl.ds(i, 256)]] for i in range(0, block_refs[0].shape[0], 256)]
    else:
        groups = [block_refs[i : i + 2] for i in range(0, len(block_refs), 2)]
    for group in groups:
        moving = jnp.concatenate([ref[...] for ref in group], axis=0)
        logits = dot(resident, moving, 1, 1) * scale_ref[0] + bias_ref[0]
        total += dot(jax.nn.sigmoid(logits).astype(BF), moving)
    own_rows, partner_rows = own_ref.shape[0], partners_ref.shape[0]
    images, texts = (partner_rows, own_rows) if turned else (own_rows, partner_rows)
    hits = jnp.where(targets_ref[...] == iota((images, texts), 0), 1.0, 0.0)
    hits = hits.T if turned else hits
    mine_ref[...] = total[:own_rows] - dot(hits.astype(BF), partners_ref[...])
    rest_ref[...] = total[own_rows:].astype(BF)


def image_back(place_ref, scale_ref, mine_ref, rest_ref, owners_ref, out_ref):
    gradient = (scale_ref[0] * (mine_ref[...] + rest_ref[...].astype(F32))).astype(BF)
    out_ref[...] = dot(requested(place_ref, owners_ref, True), gradient).astype(BF).reshape(out_ref.shape)


def text_back(scale_ref, mine_ref, rest_ref, unit_ref, norm_ref, grad_ref):
    gradient = scale_ref[0] * (mine_ref[...] + rest_ref[...].astype(F32))
    grad_ref[...] = pull_back(unit_ref[...], norm_ref[...], gradient).astype(BF)


def pool_back(received_ref, select_ref, unit_ref, norm_ref, text_ref, grad_ref, strips_ref):
    received = received_ref[...].reshape(select_ref.shape[0], -1)
    choose = select_ref[...].astype(F32).T.astype(BF)
    gradient = pull_back(unit_ref[...], norm_ref[...], dot(choose, received))
    grad_ref[...] = gradient.astype(BF)
    columns, _, strip, rows = strips_ref.shape
    turned = text_ref[...].astype(F32).T.astype(BF)
    strips_ref[:, 0] = turned.reshape(columns, strip, rows)
    turned = gradient.T.astype(BF)
    strips_ref[:, 1] = turned.reshape(columns, strip, rows)


def head_terms(place_ref, strips_ref, feats_ref, out_ref):
    yhi, core = place_ref[2], place_ref[1]
    sources, strip, lanes = strips_ref.shape
    extra = strip - lanes
    blocks = []
    for x in range(sources // 4):
        for dy in range(2):
            for dc in range(2):
                source = 4 * x + lax.rem(yhi + dy, 2) * 2 + lax.rem(core + dc, 2)
                blocks.append(strips_ref[source])
    block = jnp.concatenate(blocks, axis=1)
    block = jnp.concatenate([block[:lanes]] + [block[lanes:]] * (lanes // extra), axis=0)
    terms = dot(block, feats_ref[...])
    turned = terms.T
    turned = jnp.concatenate([turned, jnp.zeros((8, 2 * lanes), F32)], axis=0)
    row, lane = iota((8, lanes), 0), iota((8, lanes), 1)
    diagonal = (lax.div(lane, extra) == row) & (row < 5)
    for pair in range(out_ref.shape[0]):
        halves = []
        for start in (9 * pair, 9 * pair + 4):
            last = jnp.where(diagonal, turned[start : start + 8, lanes:], 0.0)
            last = jnp.sum(last, axis=0, keepdims=True)
            main = turned[start : start + 8, :lanes]
            halves.append(jnp.where(row < 5, main, jnp.where(row == 5, last, 0.0)))
        out_ref[pair] = jnp.concatenate(halves, axis=0).astype(BF)


def head_sums(place_ref, terms_ref, out_ref):
    core = place_ref[1]
    lanes = terms_ref.shape[2]
    extra = out_ref.shape[1] // 8 - lanes
    row, lane = iota((16, lanes), 0), iota((16, lanes), 1)
    diagonal = lax.div(lane, extra) == lax.rem(row, 8)
    fold = jnp.where(lax.rem(iota((lanes, extra), 0), extra) == iota((lanes, extra), 1), 1.0, 0.0)
    strips = []
    for k in range(8):
        total = terms_ref[k].astype(F32)
        for i in range(1, 16):
            total += terms_ref[8 * i + k].astype(F32)
        last = jnp.where(row < 8, total[5:6], total[13:14])
        last = jnp.where(diagonal, last, 0.0)
        last = jnp.dot(last, fold, preferred_element_type=F32, precision=lax.Precision.HIGHEST)
        strips += [total, last]
    rows = jnp.concatenate(strips, axis=1)
    to, source = iota((16, 16), 0), iota((16, 16), 1)
    order = jnp.where(2 * lax.rem(source, 8) + lax.div(source, 8) == to + core, 1.0, 0.0)
    rows = jnp.dot(order, rows, preferred_element_type=F32, precision=lax.Precision.HIGHEST)
    out_ref[...] = rows[: out_ref.shape[0]]


def per_device(
    caption_feats,
    text_head,
    image_pool,
    image_head,
    image_owner,
    image_slot,
    caption_image,
    logit_scale,
    logit_bias,
):
    captions = caption_feats[0]
    pool = image_pool[0]
    owners = image_owner[:, :, 0]
    groups, images = owners.shape
    texts, width = captions.shape
    pool_rows = pool.shape[0]
    place = jnp.stack([lax.axis_index(a) for a in (REP_AXES, "core", "yhi")])

    outs = [
        ((pool_rows, width), F32),
        ((pool_rows, 1), F32),
        ((groups, SLOTS, width), BF),
        ((groups * SLOTS, pool_rows), BF),
        ((texts, width), F32),
        ((texts, 1), F32),
        ((texts, width), BF),
    ]
    arrays = [owners, image_slot, pool, image_head, captions, text_head]
    pool_unit, pool_norm, outgoing, select, text_unit, text_norm, text_emb = pl.pallas_call(
        front,
        out_shape=[jax.ShapeDtypeStruct(s, d) for s, d in outs],
        in_specs=[SMEM] + [FAR] * len(arrays),
        out_specs=[FAR] * len(outs),
        scratch_shapes=[pltpu.VMEM(s, d) for s, d in [(a.shape, a.dtype) for a in arrays] + outs]
        + [pltpu.SemaphoreType.DMA((17,))],
        compiler_params=pltpu.CompilerParams(vmem_limit_bytes=64 * 2**20),
        name="front",
    )(place, *arrays)
    text_blocks = [lax.all_gather(text_emb, "z", axis=0, tiled=True)]
    arrived = lax.all_to_all(outgoing, REP_AXES, 0, 0, tiled=True)
    other_text = shifted(text_emb, "ylo", 1)
    keep, give = call(
        sorted_kinds, [((texts, width), BF)] * 2, "sorted_kinds", [place], [captions, pool],
        [other_text],
    )
    given = shifted(give, "core", 1)
    far_keep = shifted(keep, "yhi", 1)
    far_given = lax.ppermute(give, ("yhi", "core"), [(i, 3 - i) for i in range(4)])
    (image_emb,) = call(
        arrive, [((images, width), BF)], "arrive", [place], [arrived, owners]
    )
    other_image = shifted(image_emb, "ylo", 1)
    image_blocks = gathered_along_z(image_emb, -1)
    (feats,) = call(
        joined, [((4 * texts, width), BF)], "joined", [], [keep, given, far_keep, far_given],
        [image_blocks[3]],
    )
    feats = lax.all_gather(feats, "x", axis=0, tiled=True)

    scalars = [logit_scale, logit_bias]
    image_mine, image_rest = call(
        functools.partial(pair_sums, False),
        [((images, width), F32), ((images, width), BF)],
        "image_sums", scalars, [image_emb, other_image, caption_image, text_emb, *text_blocks],
    )
    image_sent, image_rest = image_rest, shifted(image_rest, "ylo", 1)
    (send_back,) = call(
        image_back, [((groups, SLOTS, width), BF)], "image_back",
        [place, logit_scale], [image_mine, image_rest, owners],
    )
    received = lax.all_to_all(send_back, REP_AXES, 0, 0, tiled=True)

    text_mine, text_rest = call(
        functools.partial(pair_sums, True),
        [((texts, width), F32), ((texts, width), BF)],
        "text_sums", scalars, [text_emb, other_text, caption_image, image_emb, *image_blocks],
        [image_sent],
    )
    text_rest = shifted(text_rest, "ylo", 1)
    (text_grad,) = call(
        text_back, [((texts, width), BF)], "text_back", scalars[:1],
        [text_mine, text_rest, text_unit, text_norm],
    )
    columns = groups // 2
    strip = width // columns
    pool_proj_grad, strips = call(
        pool_back,
        [((pool_rows, width), BF), ((columns, 2, strip, texts), BF)],
        "pool_back", [], [received, select, pool_unit, pool_norm, text_grad],
    )
    strips = lax.all_to_all(strips.reshape(groups, strip, texts), REP_AXES, 0, 0, tiled=True)
    text_feat_grad = dot(text_grad, text_head, 1, 1).astype(BF)
    pool_grad = dot(pool_proj_grad, image_head, 1, 1).astype(BF)

    (terms,) = call(
        head_terms, [((128, 16, 128), BF)], "head_terms", [place],
        [strips, feats],
    )
    terms = lax.all_to_all(terms.reshape(256, 8, 128), CAP_AXES + REP_AXES, 0, 0, tiled=True)
    (head_share,) = call(
        head_sums, [((9, width), F32)], "head_sums", [place], [terms.reshape(128, 16, 128)]
    )
    return text_feat_grad[None], pool_grad[None], head_share


def solution(mesh):
    fine = Mesh(mesh.devices.reshape(2, 8, 4, 2, 2), CAP_AXES + REP_AXES)
    in_specs = (
        P(REP_AXES, CAP_AXES, None),
        P(),
        P(CAP_AXES, REP_AXES, None),
        P(),
        P(None, CAP_AXES, None),
        P(None, CAP_AXES),
        P(REP_AXES, CAP_AXES),
        P(),
        P(),
    )
    out_specs = (
        P(REP_AXES, CAP_AXES, None),
        P(CAP_AXES, REP_AXES, None),
        P(CAP_AXES + REP_AXES, None),
    )
    return jax.shard_map(
        per_device, mesh=fine, in_specs=in_specs, out_specs=out_specs, check_vma=False
    )
```

```python
import functools

import jax
import jax.numpy as jnp
from jax import lax
from jax.experimental import pallas as pl
from jax.experimental.pallas import tpu as pltpu
from jax.sharding import Mesh
from jax.sharding import PartitionSpec as P

BF = jnp.bfloat16
F32 = jnp.float32
CAP_AXES = ("ylo", "z")
REP_AXES = ("x", "yhi", "core")
SLOTS = 16
FAR = pl.BlockSpec(memory_space=pltpu.HBM)
SMEM = pl.BlockSpec(memory_space=pltpu.SMEM)


def shifted(block, axis, distance):
    size = lax.axis_size(axis)
    return lax.ppermute(block, axis, [(i, (i + distance) % size) for i in range(size)])


def gathered_along_z(block, way):
    ahead, behind, found = block, block, [block]
    for _ in range(3):
        ahead, behind = shifted(ahead, "z", way), shifted(behind, "z", -way)
        found += [ahead, behind]
    return found + [shifted(ahead, "z", way)]


def together(*arrays):
    return lax.optimization_barrier(arrays)


def call(body, outs, name, scalars, arrays, after=()):
    shapes = [jax.ShapeDtypeStruct(shape, dtype) for shape, dtype in outs]
    count, total = len(arrays), len(arrays) + len(outs)

    def kernel(*refs):
        head = refs[: len(scalars)]
        far = refs[len(scalars) :][:count] + refs[len(scalars) + count + len(after) :][: len(outs)]
        near = refs[len(scalars) + len(after) + total : -1]
        sems = refs[-1]
        copies = [
            pltpu.make_async_copy(far[i], near[i], sems.at[i])
            if i < count
            else pltpu.make_async_copy(near[i], far[i], sems.at[i])
            for i in range(total)
        ]
        for i in range(count):
            copies[i].start()
        for i in range(count):
            copies[i].wait()
        body(*head, *near)
        for i in range(count, total):
            copies[i].start()
        for i in range(count, total):
            copies[i].wait()

    everything = [(a.shape, a.dtype) for a in arrays] + list(outs)
    return pl.pallas_call(
        kernel,
        out_shape=shapes,
        in_specs=[SMEM] * len(scalars) + [FAR] * (count + len(after)),
        out_specs=[FAR] * len(outs),
        scratch_shapes=[pltpu.VMEM(s, d) for s, d in everything]
        + [pltpu.SemaphoreType.DMA((total,))],
        compiler_params=pltpu.CompilerParams(vmem_limit_bytes=64 * 2**20),
        name=name,
    )(*scalars, *arrays, *after)


def dot(a, b, left=1, right=0):
    return lax.dot_general(a, b, (((left,), (right,)), ((), ())), preferred_element_type=F32)


def iota(shape, dim):
    return lax.broadcasted_iota(jnp.int32, shape, dim)


def one_hot(condition):
    return jnp.where(condition, 1.0, 0.0).astype(BF)


def pull_back(unit, norm, gradient):
    radial = jnp.sum(unit * gradient, axis=-1, keepdims=True)
    return (gradient - unit * radial) / norm


def front(
    owners_far, slots_far, pool_far, image_head_far, captions_far, text_head_far,
    pool_unit_far, pool_norm_far, out_far, select_far, text_unit_far, text_norm_far, emb_far,
    keep_far, give_far,
    owners_ref, slots_ref, pool_ref, image_head_ref, captions_ref, text_head_ref,
    pool_unit_ref, pool_norm_ref, out_ref, select_ref, text_unit_ref, text_norm_ref, emb_ref,
    keep_ref, give_ref, sems,
):
    width = pool_ref.shape[1]
    depth = width // 3
    used = [0]

    def moved(source, target):
        copy = pltpu.make_async_copy(source, target, sems.at[used[0]])
        used[0] += 1
        copy.start()
        return copy

    def cut(far, ref):
        rows = [pl.ds(i * depth, depth) for i in range(3)]
        return [moved(far.at[r], ref.at[r]) for r in rows]

    small = [moved(owners_far, owners_ref), moved(slots_far, slots_ref)]
    pool_in = moved(pool_far, pool_ref)
    image_head_in = cut(image_head_far, image_head_ref)
    captions_in = moved(captions_far, captions_ref)
    text_head_in = cut(text_head_far, text_head_ref)

    def projected(feats_ref, head_ref, head_in):
        total = jnp.zeros((feats_ref.shape[0], width), F32)
        for i in range(3):
            head_in[i].wait()
            rows = pl.ds(i * depth, depth)
            total += dot(feats_ref[:, rows], head_ref[rows])
        norm = jnp.sqrt(jnp.sum(total * total, axis=-1, keepdims=True) + 1e-06)
        return total / norm, norm

    for copy in small:
        copy.wait()
    owners = owners_ref[...]
    groups, images = owners.shape
    rows = groups * SLOTS
    owned = owners == lax.axis_index(REP_AXES)
    place = dot(one_hot(owned), one_hot(iota((images, images), 0) < iota((images, images), 1)))
    code = jnp.where(owned, place, -1.0)
    spread = one_hot(lax.div(iota((rows, groups), 0), SLOTS) == iota((rows, groups), 1))
    code_rows = dot(spread, code.astype(BF))
    slot_rows = dot(spread, slots_ref[...].astype(F32).astype(BF))
    at = lax.rem(iota((rows, images), 0), SLOTS).astype(F32)
    slot = jnp.sum(jnp.where(code_rows == at, slot_rows + 1.0, 0.0), axis=1, keepdims=True) - 1.0
    select = one_hot(slot == iota((rows, pool_ref.shape[0]), 1).astype(F32))
    select_ref[...] = select
    outs = [moved(select_ref, select_far)]

    pool_in.wait()
    unit, norm = projected(pool_ref, image_head_ref, image_head_in)
    pool_unit_ref[...] = unit
    pool_norm_ref[...] = norm
    out_ref[...] = dot(select, unit.astype(BF)).astype(BF).reshape(out_ref.shape)
    outs += [
        moved(out_ref, out_far),
        moved(pool_unit_ref, pool_unit_far),
        moved(pool_norm_ref, pool_norm_far),
    ]

    captions_in.wait()
    first = lax.axis_index("core") == 0
    keep_ref[...] = jnp.where(first, captions_ref[...], pool_ref[...])
    give_ref[...] = jnp.where(first, pool_ref[...], captions_ref[...])
    outs += [moved(keep_ref, keep_far), moved(give_ref, give_far)]
    unit, norm = projected(captions_ref, text_head_ref, text_head_in)
    emb_ref[...] = unit.astype(BF)
    outs += [moved(emb_ref, emb_far)]
    text_unit_ref[...] = unit
    text_norm_ref[...] = norm
    outs += [moved(text_unit_ref, text_unit_far), moved(text_norm_ref, text_norm_far)]
    for copy in outs:
        copy.wait()


def requested(owners_ref, turned):
    owners = owners_ref[...]
    groups, images = owners.shape
    row, lane = iota((images, images), 0), iota((images, images), 1)
    mine = jnp.sum(
        jnp.where(iota((groups, images), 0) == lax.axis_index(REP_AXES), owners.astype(F32), 0.0),
        axis=0,
        keepdims=True,
    )
    mine_t = jnp.sum(jnp.where(row == lane, mine, 0.0), axis=1, keepdims=True)
    same = mine == mine_t
    if turned:
        before = jnp.sum(jnp.where(same & (row < lane), 1.0, 0.0), axis=0, keepdims=True)
        rows = iota((groups * SLOTS, images), 0)
        return one_hot(mine * SLOTS + before == rows.astype(F32))
    before = jnp.sum(jnp.where(same & (lane < row), 1.0, 0.0), axis=1, keepdims=True)
    return one_hot(mine_t * SLOTS + before == iota((images, groups * SLOTS), 1).astype(F32))


def arrive(arrived_ref, owners_ref, emb_ref):
    hit = requested(owners_ref, False)
    emb_ref[...] = dot(hit, arrived_ref[...].reshape(hit.shape[1], -1)).astype(BF)


def joined(a_ref, b_ref, c_ref, d_ref, ab_ref, cd_ref):
    rows = a_ref.shape[0]
    ab_ref[:rows] = a_ref[...]
    ab_ref[rows:] = b_ref[...]
    cd_ref[:rows] = c_ref[...]
    cd_ref[rows:] = d_ref[...]


def pair_sums(turned, scale_ref, bias_ref, own_ref, other_ref, targets_ref, partners_ref, *refs):
    *block_refs, mine_ref, rest_ref = refs
    resident = jnp.concatenate([own_ref[...], other_ref[...]], axis=0)
    total = jnp.zeros(resident.shape, F32)
    if len(block_refs) == 1:
        groups = [[block_refs[0].at[pl.ds(i, 256)]] for i in range(0, block_refs[0].shape[0], 256)]
    else:
        groups = [block_refs[i : i + 2] for i in range(0, len(block_refs), 2)]
    for group in groups:
        moving = jnp.concatenate([ref[...] for ref in group], axis=0)
        logits = dot(resident, moving, 1, 1) * scale_ref[0] + bias_ref[0]
        total += dot(jax.nn.sigmoid(logits).astype(BF), moving)
    own_rows, partner_rows = own_ref.shape[0], partners_ref.shape[0]
    images, texts = (partner_rows, own_rows) if turned else (own_rows, partner_rows)
    hits = jnp.where(targets_ref[...] == iota((images, texts), 0), 1.0, 0.0)
    hits = hits.T if turned else hits
    mine_ref[...] = total[:own_rows] - dot(hits.astype(BF), partners_ref[...])
    rest_ref[...] = total[own_rows:].astype(BF)


def image_back(scale_ref, mine_ref, rest_ref, owners_ref, out_ref):
    gradient = (scale_ref[0] * (mine_ref[...] + rest_ref[...].astype(F32))).astype(BF)
    out_ref[...] = dot(requested(owners_ref, True), gradient).astype(BF).reshape(out_ref.shape)


def both_back(
    scale_ref, mine_ref, rest_ref, text_unit_ref, text_norm_ref,
    received_ref, select_ref, pool_unit_ref, pool_norm_ref,
    text_grad_ref, pool_grad_ref, strips_ref,
):
    columns, _, strip, rows = strips_ref.shape
    gradient = scale_ref[0] * (mine_ref[...] + rest_ref[...].astype(F32))
    gradient = pull_back(text_unit_ref[...], text_norm_ref[...], gradient)
    text_grad_ref[...] = gradient.astype(BF)
    strips_ref[:, 0] = gradient.T.astype(BF).reshape(columns, strip, rows)

    received = received_ref[...].reshape(select_ref.shape[0], -1)
    choose = select_ref[...].astype(F32).T.astype(BF)
    gradient = pull_back(pool_unit_ref[...], pool_norm_ref[...], dot(choose, received))
    pool_grad_ref[...] = gradient.astype(BF)
    strips_ref[:, 1] = gradient.T.astype(BF).reshape(columns, strip, rows)


def head_terms(strips_ref, *refs):
    x, yhi, core = (lax.axis_index(axis) for axis in REP_AXES)
    *feats_refs, out_ref = refs
    _, strip, lanes = strips_ref.shape
    extra = strip - lanes
    terms = jnp.zeros((2 * lanes, feats_refs[0].shape[1]), F32)
    for i, feats_ref in enumerate(feats_refs):
        along, across = (0, 3, 1, 2)[i // 2], i % 2
        blocks = []
        for dc in range(2):
            source = lax.rem(x + along, 4) * 4 + lax.rem(yhi + across, 2) * 2 + lax.rem(core + dc, 2)
            blocks.append(strips_ref[source])
        block = jnp.concatenate(blocks, axis=1)
        block = jnp.concatenate([block[:lanes]] + [block[lanes:]] * (lanes // extra), axis=0)
        terms += dot(block, feats_ref[...])
    turned = terms.T
    turned = jnp.concatenate([turned, jnp.zeros((8, 2 * lanes), F32)], axis=0)
    row, lane = iota((8, lanes), 0), iota((8, lanes), 1)
    diagonal = (lax.div(lane, extra) == row) & (row < 5)
    for pair in range(out_ref.shape[0]):
        halves = []
        for start in (9 * pair, 9 * pair + 4):
            last = jnp.where(diagonal, turned[start : start + 8, lanes:], 0.0)
            last = jnp.sum(last, axis=0, keepdims=True)
            main = turned[start : start + 8, :lanes]
            halves.append(jnp.where(row < 5, main, jnp.where(row == 5, last, 0.0)))
        out_ref[pair] = jnp.concatenate(halves, axis=0).astype(BF)


def head_sums(terms_ref, out_ref):
    core = lax.axis_index("core")
    lanes = terms_ref.shape[2]
    extra = out_ref.shape[1] // 8 - lanes
    row, lane = iota((16, lanes), 0), iota((16, lanes), 1)
    diagonal = lax.div(lane, extra) == lax.rem(row, 8)
    fold = jnp.where(lax.rem(iota((lanes, extra), 0), extra) == iota((lanes, extra), 1), 1.0, 0.0)
    strips = []
    for k in range(8):
        total = terms_ref[k].astype(F32)
        for i in range(1, 16):
            total += terms_ref[8 * i + k].astype(F32)
        last = jnp.where(row < 8, total[5:6], total[13:14])
        last = jnp.where(diagonal, last, 0.0)
        last = jnp.dot(last, fold, preferred_element_type=F32, precision=lax.Precision.HIGHEST)
        strips += [total, last]
    rows = jnp.concatenate(strips, axis=1)
    to, source = iota((16, 16), 0), iota((16, 16), 1)
    order = jnp.where(2 * lax.rem(source, 8) + lax.div(source, 8) == to + core, 1.0, 0.0)
    rows = jnp.dot(order, rows, preferred_element_type=F32, precision=lax.Precision.HIGHEST)
    out_ref[...] = rows[: out_ref.shape[0]]


def per_device(
    caption_feats,
    text_head,
    image_pool,
    image_head,
    image_owner,
    image_slot,
    caption_image,
    logit_scale,
    logit_bias,
):
    captions = caption_feats[0]
    pool = image_pool[0]
    owners = image_owner[:, :, 0]
    groups, images = owners.shape
    texts, width = captions.shape
    pool_rows = pool.shape[0]
    outs = [
        ((pool_rows, width), F32),
        ((pool_rows, 1), F32),
        ((groups, SLOTS, width), BF),
        ((groups * SLOTS, pool_rows), BF),
        ((texts, width), F32),
        ((texts, 1), F32),
        ((texts, width), BF),
        ((texts, width), BF),
        ((texts, width), BF),
    ]
    arrays = [owners, image_slot, pool, image_head, captions, text_head]
    pool_unit, pool_norm, outgoing, select, text_unit, text_norm, text_emb, keep, give = pl.pallas_call(
        front,
        out_shape=[jax.ShapeDtypeStruct(s, d) for s, d in outs],
        in_specs=[FAR] * len(arrays),
        out_specs=[FAR] * len(outs),
        scratch_shapes=[pltpu.VMEM(s, d) for s, d in [(a.shape, a.dtype) for a in arrays] + outs]
        + [pltpu.SemaphoreType.DMA((19,))],
        compiler_params=pltpu.CompilerParams(vmem_limit_bytes=64 * 2**20),
        name="front",
    )(*arrays)
    text_blocks = gathered_along_z(text_emb, 1)
    arrived = lax.all_to_all(outgoing, REP_AXES, 0, 0, tiled=True)
    other_text = shifted(text_emb, "ylo", 1)
    given = shifted(give, "core", 1)
    far_keep = shifted(keep, "yhi", 1)
    far_given = lax.ppermute(give, ("yhi", "core"), [(i, 3 - i) for i in range(4)])
    (image_emb,) = call(
        arrive, [((images, width), BF)], "arrive", [], [arrived, owners], [given]
    )
    other_image = shifted(image_emb, "ylo", 1)
    image_blocks = [image_emb]
    ahead = behind = image_emb
    for step in range(3):
        ahead, behind = shifted(ahead, "z", -1), shifted(behind, "z", 1)
        ahead, behind = together(ahead, behind)
        image_blocks += [ahead, behind]
    image_blocks += [shifted(ahead, "z", -1)]
    home, far = call(
        joined, [((2 * texts, width), BF)] * 2, "joined", [], [keep, given, far_keep, far_given],
    )
    feats = [home, far]
    feats += [shifted(home, "x", 1), shifted(far, "x", 1)]
    feats += [shifted(home, "x", -1), shifted(far, "x", -1)]
    feats += [shifted(feats[2], "x", 1), shifted(feats[5], "x", -1)]

    scalars = [logit_scale, logit_bias]
    image_mine, image_rest = call(
        functools.partial(pair_sums, False),
        [((images, width), F32), ((images, width), BF)],
        "image_sums", scalars, [image_emb, other_image, caption_image, text_emb, *text_blocks],
        [home],
    )
    image_sent, image_rest = image_rest, shifted(image_rest, "ylo", 1)
    (send_back,) = call(
        image_back, [((groups, SLOTS, width), BF)], "image_back",
        [logit_scale], [image_mine, image_rest, owners],
        [feats[2], feats[4], *image_blocks[6:]],
    )
    received = lax.all_to_all(send_back, REP_AXES, 0, 0, tiled=True)

    text_mine, text_rest = call(
        functools.partial(pair_sums, True),
        [((texts, width), F32), ((texts, width), BF)],
        "text_sums", scalars, [text_emb, other_text, caption_image, image_emb, *image_blocks],
        [send_back, feats[3], feats[5]],
    )
    text_rest = shifted(text_rest, "ylo", 1)
    columns = groups // 2
    strip = width // columns
    text_grad, pool_proj_grad, strips = call(
        both_back,
        [((texts, width), BF), ((pool_rows, width), BF), ((columns, 2, strip, texts), BF)],
        "both_back", scalars[:1],
        [text_mine, text_rest, text_unit, text_norm, received, select, pool_unit, pool_norm],
    )
    strips = lax.all_to_all(strips.reshape(groups, strip, texts), REP_AXES, 0, 0, tiled=True)
    text_feat_grad = dot(text_grad, text_head, 1, 1).astype(BF)
    pool_grad = dot(pool_proj_grad, image_head, 1, 1).astype(BF)

    (terms,) = call(
        head_terms, [((128, 16, 128), BF)], "head_terms", [],
        [strips, *feats],
    )
    terms = lax.all_to_all(terms.reshape(256, 8, 128), CAP_AXES + REP_AXES, 0, 0, tiled=True)
    (head_share,) = call(
        head_sums, [((9, width), F32)], "head_sums", [], [terms.reshape(128, 16, 128)]
    )
    return text_feat_grad[None], pool_grad[None], head_share


def solution(mesh):
    fine = Mesh(mesh.devices.reshape(2, 8, 4, 2, 2), CAP_AXES + REP_AXES)
    in_specs = (
        P(REP_AXES, CAP_AXES, None),
        P(),
        P(CAP_AXES, REP_AXES, None),
        P(),
        P(None, CAP_AXES, None),
        P(None, CAP_AXES),
        P(REP_AXES, CAP_AXES),
        P(),
        P(),
    )
    out_specs = (
        P(REP_AXES, CAP_AXES, None),
        P(CAP_AXES, REP_AXES, None),
        P(CAP_AXES + REP_AXES, None),
    )
    return jax.shard_map(
        per_device, mesh=fine, in_specs=in_specs, out_specs=out_specs, check_vma=False
    )
```

```python
import functools

import jax
import jax.numpy as jnp
from jax import lax
from jax.experimental import pallas as pl
from jax.experimental.pallas import tpu as pltpu
from jax.sharding import Mesh
from jax.sharding import PartitionSpec as P

BF = jnp.bfloat16
F32 = jnp.float32
CAP_AXES = ("ylo", "z")
REP_AXES = ("x", "yhi", "core")
SLOTS = 16
FAR = pl.BlockSpec(memory_space=pltpu.HBM)
SMEM = pl.BlockSpec(memory_space=pltpu.SMEM)


def shifted(block, axis, distance):
    size = lax.axis_size(axis)
    return lax.ppermute(block, axis, [(i, (i + distance) % size) for i in range(size)])


def gathered_along_z(block, way):
    ahead, behind, found = block, block, [block]
    for _ in range(3):
        ahead, behind = shifted(ahead, "z", way), shifted(behind, "z", -way)
        found += [ahead, behind]
    return found + [shifted(ahead, "z", way)]


def together(*arrays):
    return lax.optimization_barrier(arrays)


def call(body, outs, name, scalars, arrays, after=()):
    shapes = [jax.ShapeDtypeStruct(shape, dtype) for shape, dtype in outs]
    count, total = len(arrays), len(arrays) + len(outs)

    def kernel(*refs):
        head = refs[: len(scalars)]
        far = refs[len(scalars) :][:count] + refs[len(scalars) + count + len(after) :][: len(outs)]
        near = refs[len(scalars) + len(after) + total : -1]
        sems = refs[-1]
        copies = [
            pltpu.make_async_copy(far[i], near[i], sems.at[i])
            if i < count
            else pltpu.make_async_copy(near[i], far[i], sems.at[i])
            for i in range(total)
        ]
        for i in range(count):
            copies[i].start()
        for i in range(count):
            copies[i].wait()
        body(*head, *near)
        for i in range(count, total):
            copies[i].start()
        for i in range(count, total):
            copies[i].wait()

    everything = [(a.shape, a.dtype) for a in arrays] + list(outs)
    return pl.pallas_call(
        kernel,
        out_shape=shapes,
        in_specs=[SMEM] * len(scalars) + [FAR] * (count + len(after)),
        out_specs=[FAR] * len(outs),
        scratch_shapes=[pltpu.VMEM(s, d) for s, d in everything]
        + [pltpu.SemaphoreType.DMA((total,))],
        compiler_params=pltpu.CompilerParams(vmem_limit_bytes=64 * 2**20),
        name=name,
    )(*scalars, *arrays, *after)


def dot(a, b, left=1, right=0):
    return lax.dot_general(a, b, (((left,), (right,)), ((), ())), preferred_element_type=F32)


def iota(shape, dim):
    return lax.broadcasted_iota(jnp.int32, shape, dim)


def one_hot(condition):
    return jnp.where(condition, 1.0, 0.0).astype(BF)


def pull_back(unit, norm, gradient):
    radial = jnp.sum(unit * gradient, axis=-1, keepdims=True)
    return (gradient - unit * radial) / norm


def front(
    owners_far, slots_far, pool_far, image_head_far, captions_far, text_head_far,
    pool_unit_far, pool_norm_far, out_far, select_far, text_unit_far, text_norm_far, emb_far,
    keep_far, give_far,
    owners_ref, slots_ref, pool_ref, image_head_ref, captions_ref, text_head_ref,
    pool_unit_ref, pool_norm_ref, out_ref, select_ref, text_unit_ref, text_norm_ref, emb_ref,
    keep_ref, give_ref, sems,
):
    width = pool_ref.shape[1]
    depth = width // 3
    used = [0]

    def moved(source, target):
        copy = pltpu.make_async_copy(source, target, sems.at[used[0]])
        used[0] += 1
        copy.start()
        return copy

    def cut(far, ref):
        rows = [pl.ds(i * depth, depth) for i in range(3)]
        return [moved(far.at[r], ref.at[r]) for r in rows]

    small = [moved(owners_far, owners_ref), moved(slots_far, slots_ref)]
    pool_in = moved(pool_far, pool_ref)
    image_head_in = cut(image_head_far, image_head_ref)
    captions_in = moved(captions_far, captions_ref)
    text_head_in = cut(text_head_far, text_head_ref)

    def projected(feats_ref, head_ref, head_in):
        total = jnp.zeros((feats_ref.shape[0], width), F32)
        for i in range(3):
            head_in[i].wait()
            rows = pl.ds(i * depth, depth)
            total += dot(feats_ref[:, rows], head_ref[rows])
        norm = jnp.sqrt(jnp.sum(total * total, axis=-1, keepdims=True) + 1e-06)
        return total / norm, norm

    for copy in small:
        copy.wait()
    owners = owners_ref[...]
    groups, images = owners.shape
    rows = groups * SLOTS
    owned = owners == lax.axis_index(REP_AXES)
    place = dot(one_hot(owned), one_hot(iota((images, images), 0) < iota((images, images), 1)))
    code = jnp.where(owned, place, -1.0)
    spread = one_hot(lax.div(iota((rows, groups), 0), SLOTS) == iota((rows, groups), 1))
    code_rows = dot(spread, code.astype(BF))
    slot_rows = dot(spread, slots_ref[...].astype(F32).astype(BF))
    at = lax.rem(iota((rows, images), 0), SLOTS).astype(F32)
    slot = jnp.sum(jnp.where(code_rows == at, slot_rows + 1.0, 0.0), axis=1, keepdims=True) - 1.0
    select = one_hot(slot == iota((rows, pool_ref.shape[0]), 1).astype(F32))
    select_ref[...] = select
    outs = [moved(select_ref, select_far)]

    pool_in.wait()
    unit, norm = projected(pool_ref, image_head_ref, image_head_in)
    pool_unit_ref[...] = unit
    pool_norm_ref[...] = norm
    out_ref[...] = dot(select, unit.astype(BF)).astype(BF).reshape(out_ref.shape)
    outs += [
        moved(out_ref, out_far),
        moved(pool_unit_ref, pool_unit_far),
        moved(pool_norm_ref, pool_norm_far),
    ]

    captions_in.wait()
    first = lax.axis_index("core") == 0
    keep_ref[...] = jnp.where(first, captions_ref[...], pool_ref[...])
    give_ref[...] = jnp.where(first, pool_ref[...], captions_ref[...])
    outs += [moved(keep_ref, keep_far), moved(give_ref, give_far)]
    unit, norm = projected(captions_ref, text_head_ref, text_head_in)
    emb_ref[...] = unit.astype(BF)
    outs += [moved(emb_ref, emb_far)]
    text_unit_ref[...] = unit
    text_norm_ref[...] = norm
    outs += [moved(text_unit_ref, text_unit_far), moved(text_norm_ref, text_norm_far)]
    for copy in outs:
        copy.wait()


def requested(owners_ref, turned):
    owners = owners_ref[...]
    groups, images = owners.shape
    row, lane = iota((images, images), 0), iota((images, images), 1)
    mine = jnp.sum(
        jnp.where(iota((groups, images), 0) == lax.axis_index(REP_AXES), owners.astype(F32), 0.0),
        axis=0,
        keepdims=True,
    )
    mine_t = jnp.sum(jnp.where(row == lane, mine, 0.0), axis=1, keepdims=True)
    same = mine == mine_t
    if turned:
        before = jnp.sum(jnp.where(same & (row < lane), 1.0, 0.0), axis=0, keepdims=True)
        rows = iota((groups * SLOTS, images), 0)
        return one_hot(mine * SLOTS + before == rows.astype(F32))
    before = jnp.sum(jnp.where(same & (lane < row), 1.0, 0.0), axis=1, keepdims=True)
    return one_hot(mine_t * SLOTS + before == iota((images, groups * SLOTS), 1).astype(F32))


def arrive(arrived_ref, owners_ref, emb_ref):
    hit = requested(owners_ref, False)
    emb_ref[...] = dot(hit, arrived_ref[...].reshape(hit.shape[1], -1)).astype(BF)


def joined(a_ref, b_ref, c_ref, d_ref, ab_ref, cd_ref):
    rows = a_ref.shape[0]
    ab_ref[:rows] = a_ref[...]
    ab_ref[rows:] = b_ref[...]
    cd_ref[:rows] = c_ref[...]
    cd_ref[rows:] = d_ref[...]


def pair_sums(turned, count, scale_ref, bias_ref, targets_far, own_far, other_far, *refs):
    blocks_far = refs[:count]
    mine_far, rest_far, targets_ref, resident_ref, moving_ref, mine_ref, rest_ref, sems = refs[-8:]
    used = 0
    copies = []
    for far, ref in ((own_far, resident_ref), (other_far, resident_ref), (targets_far, targets_ref)):
        part = ref.at[pl.ds(own_far.shape[0], own_far.shape[0])] if far is other_far else ref
        part = ref.at[pl.ds(0, own_far.shape[0])] if far is own_far else part
        copies.append(pltpu.make_async_copy(far, part, sems.at[len(copies)]))
        copies[-1].start()
    for far in blocks_far:
        rows = far.shape[0]
        part = moving_ref.at[pl.ds(used, rows)]
        copies.append(pltpu.make_async_copy(far, part, sems.at[len(copies)]))
        copies[-1].start()
        used += rows
    for copy in copies:
        copy.wait()
    resident, moving = resident_ref[...], moving_ref[...]
    logits = dot(resident, moving, 1, 1) * scale_ref[0] + bias_ref[0]
    total = dot(jax.nn.sigmoid(logits).astype(BF), moving)
    own_rows, partner_rows = mine_ref.shape[0], blocks_far[0].shape[0]
    images, texts = (partner_rows, own_rows) if turned else (own_rows, partner_rows)
    hits = jnp.where(targets_ref[...] == iota((images, texts), 0), 1.0, 0.0)
    hits = hits.T if turned else hits
    mine_ref[...] = total[:own_rows] - dot(hits.astype(BF), moving_ref[:partner_rows])
    rest_ref[...] = total[own_rows:].astype(BF)
    outs = [
        pltpu.make_async_copy(mine_ref, mine_far, sems.at[len(copies)]),
        pltpu.make_async_copy(rest_ref, rest_far, sems.at[len(copies) + 1]),
    ]
    for copy in outs:
        copy.start()
    for copy in outs:
        copy.wait()


def pair_call(turned, name, scalars, targets, own, other, blocks, after):
    rows, width = own.shape
    moving = (sum(block.shape[0] for block in blocks), width)
    arrays = [targets, own, other, *blocks]
    return pl.pallas_call(
        functools.partial(pair_sums, turned, len(blocks)),
        out_shape=[jax.ShapeDtypeStruct((rows, width), d) for d in (F32, BF)],
        in_specs=[SMEM] * 2 + [FAR] * (len(arrays) + len(after)),
        out_specs=[FAR] * 2,
        scratch_shapes=[
            pltpu.VMEM(targets.shape, targets.dtype),
            pltpu.VMEM((2 * rows, width), BF),
            pltpu.VMEM(moving, BF),
            pltpu.VMEM((rows, width), F32),
            pltpu.VMEM((rows, width), BF),
            pltpu.SemaphoreType.DMA((len(arrays) + 2,)),
        ],
        compiler_params=pltpu.CompilerParams(vmem_limit_bytes=64 * 2**20),
        name=name,
    )(*scalars, *arrays, *after)


def image_back(scale_ref, mine_ref, rest_ref, owners_ref, out_ref):
    gradient = (scale_ref[0] * (mine_ref[...] + rest_ref[...].astype(F32))).astype(BF)
    out_ref[...] = dot(requested(owners_ref, True), gradient).astype(BF).reshape(out_ref.shape)


def both_back(
    scale_ref, mine_ref, rest_ref, text_unit_ref, text_norm_ref,
    received_ref, select_ref, pool_unit_ref, pool_norm_ref,
    text_grad_ref, pool_grad_ref, strips_ref,
):
    columns, _, strip, rows = strips_ref.shape
    gradient = scale_ref[0] * (mine_ref[...] + rest_ref[...].astype(F32))
    gradient = pull_back(text_unit_ref[...], text_norm_ref[...], gradient)
    text_grad_ref[...] = gradient.astype(BF)
    strips_ref[:, 0] = gradient.T.astype(BF).reshape(columns, strip, rows)

    received = received_ref[...].reshape(select_ref.shape[0], -1)
    choose = select_ref[...].astype(F32).T.astype(BF)
    gradient = pull_back(pool_unit_ref[...], pool_norm_ref[...], dot(choose, received))
    pool_grad_ref[...] = gradient.astype(BF)
    strips_ref[:, 1] = gradient.T.astype(BF).reshape(columns, strip, rows)


def head_terms(strips_ref, *refs):
    x, yhi, core = (lax.axis_index(axis) for axis in REP_AXES)
    *feats_refs, out_ref = refs
    _, strip, lanes = strips_ref.shape
    extra = strip - lanes
    terms = jnp.zeros((2 * lanes, feats_refs[0].shape[1]), F32)
    for i, feats_ref in enumerate(feats_refs):
        along, across = (0, 3, 1, 2)[i // 2], i % 2
        blocks = []
        for dc in range(2):
            source = lax.rem(x + along, 4) * 4 + lax.rem(yhi + across, 2) * 2 + lax.rem(core + dc, 2)
            blocks.append(strips_ref[source])
        block = jnp.concatenate(blocks, axis=1)
        block = jnp.concatenate([block[:lanes]] + [block[lanes:]] * (lanes // extra), axis=0)
        terms += dot(block, feats_ref[...])
    turned = terms.T
    turned = jnp.concatenate([turned, jnp.zeros((8, 2 * lanes), F32)], axis=0)
    row, lane = iota((8, lanes), 0), iota((8, lanes), 1)
    diagonal = (lax.div(lane, extra) == row) & (row < 5)
    for pair in range(out_ref.shape[0]):
        halves = []
        for start in (9 * pair, 9 * pair + 4):
            last = jnp.where(diagonal, turned[start : start + 8, lanes:], 0.0)
            last = jnp.sum(last, axis=0, keepdims=True)
            main = turned[start : start + 8, :lanes]
            halves.append(jnp.where(row < 5, main, jnp.where(row == 5, last, 0.0)))
        out_ref[pair] = jnp.concatenate(halves, axis=0).astype(BF)


def head_sums(terms_ref, out_ref):
    core = lax.axis_index("core")
    lanes = terms_ref.shape[2]
    extra = out_ref.shape[1] // 8 - lanes
    row, lane = iota((16, lanes), 0), iota((16, lanes), 1)
    diagonal = lax.div(lane, extra) == lax.rem(row, 8)
    fold = jnp.where(lax.rem(iota((lanes, extra), 0), extra) == iota((lanes, extra), 1), 1.0, 0.0)
    strips = []
    for k in range(8):
        total = terms_ref[k].astype(F32)
        for i in range(1, 16):
            total += terms_ref[8 * i + k].astype(F32)
        last = jnp.where(row < 8, total[5:6], total[13:14])
        last = jnp.where(diagonal, last, 0.0)
        last = jnp.dot(last, fold, preferred_element_type=F32, precision=lax.Precision.HIGHEST)
        strips += [total, last]
    rows = jnp.concatenate(strips, axis=1)
    to, source = iota((16, 16), 0), iota((16, 16), 1)
    order = jnp.where(2 * lax.rem(source, 8) + lax.div(source, 8) == to + core, 1.0, 0.0)
    rows = jnp.dot(order, rows, preferred_element_type=F32, precision=lax.Precision.HIGHEST)
    out_ref[...] = rows[: out_ref.shape[0]]


def per_device(
    caption_feats,
    text_head,
    image_pool,
    image_head,
    image_owner,
    image_slot,
    caption_image,
    logit_scale,
    logit_bias,
):
    captions = caption_feats[0]
    pool = image_pool[0]
    owners = image_owner[:, :, 0]
    groups, images = owners.shape
    texts, width = captions.shape
    pool_rows = pool.shape[0]
    outs = [
        ((pool_rows, width), F32),
        ((pool_rows, 1), F32),
        ((groups, SLOTS, width), BF),
        ((groups * SLOTS, pool_rows), BF),
        ((texts, width), F32),
        ((texts, 1), F32),
        ((texts, width), BF),
        ((texts, width), BF),
        ((texts, width), BF),
    ]
    arrays = [owners, image_slot, pool, image_head, captions, text_head]
    pool_unit, pool_norm, outgoing, select, text_unit, text_norm, text_emb, keep, give = pl.pallas_call(
        front,
        out_shape=[jax.ShapeDtypeStruct(s, d) for s, d in outs],
        in_specs=[FAR] * len(arrays),
        out_specs=[FAR] * len(outs),
        scratch_shapes=[pltpu.VMEM(s, d) for s, d in [(a.shape, a.dtype) for a in arrays] + outs]
        + [pltpu.SemaphoreType.DMA((19,))],
        compiler_params=pltpu.CompilerParams(vmem_limit_bytes=64 * 2**20),
        name="front",
    )(*arrays)
    text_blocks = gathered_along_z(text_emb, 1)
    arrived = lax.all_to_all(outgoing, REP_AXES, 0, 0, tiled=True)
    other_text = shifted(text_emb, "ylo", 1)
    given = shifted(give, "core", 1)
    far_keep = shifted(keep, "yhi", 1)
    far_given = lax.ppermute(give, ("yhi", "core"), [(i, 3 - i) for i in range(4)])
    (image_emb,) = call(
        arrive, [((images, width), BF)], "arrive", [], [arrived, owners], [given]
    )
    other_image = shifted(image_emb, "ylo", 1)
    image_blocks = [image_emb]
    ahead = behind = image_emb
    for step in range(3):
        ahead, behind = shifted(ahead, "z", -1), shifted(behind, "z", 1)
        ahead, behind = together(ahead, behind)
        image_blocks += [ahead, behind]
    image_blocks += [shifted(ahead, "z", -1)]
    home, far = call(
        joined, [((2 * texts, width), BF)] * 2, "joined", [], [keep, given, far_keep, far_given],
    )
    feats = [home, far]
    feats += [shifted(home, "x", 1), shifted(far, "x", 1)]
    feats += [shifted(home, "x", -1), shifted(far, "x", -1)]
    feats += [shifted(feats[2], "x", 1), shifted(feats[5], "x", -1)]

    scalars = [logit_scale, logit_bias]
    image_mine, image_rest = pair_call(
        False, "image_sums", scalars, caption_image, image_emb, other_image, text_blocks, [home]
    )
    image_sent, image_rest = image_rest, shifted(image_rest, "ylo", 1)
    (send_back,) = call(
        image_back, [((groups, SLOTS, width), BF)], "image_back",
        [logit_scale], [image_mine, image_rest, owners],
        [feats[2], feats[4], *image_blocks[6:]],
    )
    received = lax.all_to_all(send_back, REP_AXES, 0, 0, tiled=True)

    text_mine, text_rest = pair_call(
        True, "text_sums", scalars, caption_image, text_emb, other_text, image_blocks,
        [send_back, feats[3], feats[5]],
    )
    text_rest = shifted(text_rest, "ylo", 1)
    columns = groups // 2
    strip = width // columns
    text_grad, pool_proj_grad, strips = call(
        both_back,
        [((texts, width), BF), ((pool_rows, width), BF), ((columns, 2, strip, texts), BF)],
        "both_back", scalars[:1],
        [text_mine, text_rest, text_unit, text_norm, received, select, pool_unit, pool_norm],
    )
    strips = lax.all_to_all(strips.reshape(groups, strip, texts), REP_AXES, 0, 0, tiled=True)
    text_feat_grad = dot(text_grad, text_head, 1, 1).astype(BF)
    pool_grad = dot(pool_proj_grad, image_head, 1, 1).astype(BF)

    (terms,) = call(
        head_terms, [((128, 16, 128), BF)], "head_terms", [],
        [strips, *feats],
    )
    terms = lax.all_to_all(terms.reshape(256, 8, 128), CAP_AXES + REP_AXES, 0, 0, tiled=True)
    (head_share,) = call(
        head_sums, [((9, width), F32)], "head_sums", [], [terms.reshape(128, 16, 128)]
    )
    return text_feat_grad[None], pool_grad[None], head_share


def solution(mesh):
    fine = Mesh(mesh.devices.reshape(2, 8, 4, 2, 2), CAP_AXES + REP_AXES)
    in_specs = (
        P(REP_AXES, CAP_AXES, None),
        P(),
        P(CAP_AXES, REP_AXES, None),
        P(),
        P(None, CAP_AXES, None),
        P(None, CAP_AXES),
        P(REP_AXES, CAP_AXES),
        P(),
        P(),
    )
    out_specs = (
        P(REP_AXES, CAP_AXES, None),
        P(CAP_AXES, REP_AXES, None),
        P(CAP_AXES + REP_AXES, None),
    )
    return jax.shard_map(
        per_device, mesh=fine, in_specs=in_specs, out_specs=out_specs, check_vma=False
    )
```

```python
import functools

import jax
import jax.numpy as jnp
from jax import lax
from jax.experimental import pallas as pl
from jax.experimental.pallas import tpu as pltpu
from jax.sharding import Mesh
from jax.sharding import PartitionSpec as P

BF = jnp.bfloat16
F32 = jnp.float32
CAP_AXES = ("ylo", "z")
REP_AXES = ("x", "yhi", "core")
SLOTS = 16
FAR = pl.BlockSpec(memory_space=pltpu.HBM)
SMEM = pl.BlockSpec(memory_space=pltpu.SMEM)


def shifted(block, axis, distance):
    size = lax.axis_size(axis)
    return lax.ppermute(block, axis, [(i, (i + distance) % size) for i in range(size)])


def gathered_along_z(block, way):
    ahead, behind, found = block, block, [block]
    for _ in range(3):
        ahead, behind = shifted(ahead, "z", way), shifted(behind, "z", -way)
        found += [ahead, behind]
    return found + [shifted(ahead, "z", way)]


def together(*arrays):
    return lax.optimization_barrier(arrays)


def call(body, outs, name, scalars, arrays, after=()):
    shapes = [jax.ShapeDtypeStruct(shape, dtype) for shape, dtype in outs]
    count, total = len(arrays), len(arrays) + len(outs)

    def kernel(*refs):
        head = refs[: len(scalars)]
        far = refs[len(scalars) :][:count] + refs[len(scalars) + count + len(after) :][: len(outs)]
        near = refs[len(scalars) + len(after) + total : -1]
        sems = refs[-1]
        copies = [
            pltpu.make_async_copy(far[i], near[i], sems.at[i])
            if i < count
            else pltpu.make_async_copy(near[i], far[i], sems.at[i])
            for i in range(total)
        ]
        for i in range(count):
            copies[i].start()
        for i in range(count):
            copies[i].wait()
        body(*head, *near)
        for i in range(count, total):
            copies[i].start()
        for i in range(count, total):
            copies[i].wait()

    everything = [(a.shape, a.dtype) for a in arrays] + list(outs)
    return pl.pallas_call(
        kernel,
        out_shape=shapes,
        in_specs=[SMEM] * len(scalars) + [FAR] * (count + len(after)),
        out_specs=[FAR] * len(outs),
        scratch_shapes=[pltpu.VMEM(s, d) for s, d in everything]
        + [pltpu.SemaphoreType.DMA((total,))],
        compiler_params=pltpu.CompilerParams(vmem_limit_bytes=64 * 2**20),
        name=name,
    )(*scalars, *arrays, *after)


def dot(a, b, left=1, right=0):
    return lax.dot_general(a, b, (((left,), (right,)), ((), ())), preferred_element_type=F32)


def iota(shape, dim):
    return lax.broadcasted_iota(jnp.int32, shape, dim)


def one_hot(condition):
    return jnp.where(condition, 1.0, 0.0).astype(BF)


def pull_back(unit, norm, gradient):
    radial = jnp.sum(unit * gradient, axis=-1, keepdims=True)
    return (gradient - unit * radial) / norm


def front(
    owners_far, slots_far, pool_far, image_head_far, captions_far, text_head_far,
    pool_unit_far, pool_norm_far, out_far, select_far, text_unit_far, text_norm_far, emb_far,
    keep_far, give_far,
    owners_ref, slots_ref, pool_ref, image_head_ref, captions_ref, text_head_ref,
    pool_unit_ref, pool_norm_ref, out_ref, select_ref, text_unit_ref, text_norm_ref, emb_ref,
    keep_ref, give_ref, sems,
):
    width = pool_ref.shape[1]
    depth = width // 3
    used = [0]

    def moved(source, target):
        copy = pltpu.make_async_copy(source, target, sems.at[used[0]])
        used[0] += 1
        copy.start()
        return copy

    def cut(far, ref):
        rows = [pl.ds(i * depth, depth) for i in range(3)]
        return [moved(far.at[r], ref.at[r]) for r in rows]

    small = [moved(owners_far, owners_ref), moved(slots_far, slots_ref)]
    pool_in = moved(pool_far, pool_ref)
    image_head_in = cut(image_head_far, image_head_ref)
    captions_in = moved(captions_far, captions_ref)
    text_head_in = cut(text_head_far, text_head_ref)

    def projected(feats_ref, head_ref, head_in):
        total = jnp.zeros((feats_ref.shape[0], width), F32)
        for i in range(3):
            head_in[i].wait()
            rows = pl.ds(i * depth, depth)
            total += dot(feats_ref[:, rows], head_ref[rows])
        norm = jnp.sqrt(jnp.sum(total * total, axis=-1, keepdims=True) + 1e-06)
        return total / norm, norm

    for copy in small:
        copy.wait()
    owners = owners_ref[...]
    groups, images = owners.shape
    rows = groups * SLOTS
    owned = owners == lax.axis_index(REP_AXES)
    place = dot(one_hot(owned), one_hot(iota((images, images), 0) < iota((images, images), 1)))
    code = jnp.where(owned, place, -1.0)
    spread = one_hot(lax.div(iota((rows, groups), 0), SLOTS) == iota((rows, groups), 1))
    code_rows = dot(spread, code.astype(BF))
    slot_rows = dot(spread, slots_ref[...].astype(F32).astype(BF))
    at = lax.rem(iota((rows, images), 0), SLOTS).astype(F32)
    slot = jnp.sum(jnp.where(code_rows == at, slot_rows + 1.0, 0.0), axis=1, keepdims=True) - 1.0
    select = one_hot(slot == iota((rows, pool_ref.shape[0]), 1).astype(F32))
    select_ref[...] = select
    outs = [moved(select_ref, select_far)]

    pool_in.wait()
    unit, norm = projected(pool_ref, image_head_ref, image_head_in)
    pool_unit_ref[...] = unit
    pool_norm_ref[...] = norm
    out_ref[...] = dot(select, unit.astype(BF)).astype(BF).reshape(out_ref.shape)
    outs += [
        moved(out_ref, out_far),
        moved(pool_unit_ref, pool_unit_far),
        moved(pool_norm_ref, pool_norm_far),
    ]

    captions_in.wait()
    first = lax.axis_index("core") == 0
    keep_ref[...] = jnp.where(first, captions_ref[...], pool_ref[...])
    give_ref[...] = jnp.where(first, pool_ref[...], captions_ref[...])
    outs += [moved(keep_ref, keep_far), moved(give_ref, give_far)]
    unit, norm = projected(captions_ref, text_head_ref, text_head_in)
    emb_ref[...] = unit.astype(BF)
    outs += [moved(emb_ref, emb_far)]
    text_unit_ref[...] = unit
    text_norm_ref[...] = norm
    outs += [moved(text_unit_ref, text_unit_far), moved(text_norm_ref, text_norm_far)]
    for copy in outs:
        copy.wait()


def requested(owners_ref, turned):
    owners = owners_ref[...]
    groups, images = owners.shape
    row, lane = iota((images, images), 0), iota((images, images), 1)
    mine = jnp.sum(
        jnp.where(iota((groups, images), 0) == lax.axis_index(REP_AXES), owners.astype(F32), 0.0),
        axis=0,
        keepdims=True,
    )
    mine_t = jnp.sum(jnp.where(row == lane, mine, 0.0), axis=1, keepdims=True)
    same = mine == mine_t
    if turned:
        before = jnp.sum(jnp.where(same & (row < lane), 1.0, 0.0), axis=0, keepdims=True)
        rows = iota((groups * SLOTS, images), 0)
        return one_hot(mine * SLOTS + before == rows.astype(F32))
    before = jnp.sum(jnp.where(same & (lane < row), 1.0, 0.0), axis=1, keepdims=True)
    return one_hot(mine_t * SLOTS + before == iota((images, groups * SLOTS), 1).astype(F32))


def arrive(arrived_ref, owners_ref, emb_ref):
    hit = requested(owners_ref, False)
    emb_ref[...] = dot(hit, arrived_ref[...].reshape(hit.shape[1], -1)).astype(BF)


def joined(a_ref, b_ref, c_ref, d_ref, ab_ref, cd_ref):
    rows = a_ref.shape[0]
    ab_ref[:rows] = a_ref[...]
    ab_ref[rows:] = b_ref[...]
    cd_ref[:rows] = c_ref[...]
    cd_ref[rows:] = d_ref[...]


def pair_sums(turned, count, scale_ref, bias_ref, targets_far, own_far, other_far, *refs):
    blocks_far = refs[:count]
    mine_far, rest_far, targets_ref, resident_ref, moving_ref, mine_ref, rest_ref, sems = refs[-8:]
    used = 0
    copies = []
    for far, ref in ((own_far, resident_ref), (other_far, resident_ref), (targets_far, targets_ref)):
        part = ref.at[pl.ds(own_far.shape[0], own_far.shape[0])] if far is other_far else ref
        part = ref.at[pl.ds(0, own_far.shape[0])] if far is own_far else part
        copies.append(pltpu.make_async_copy(far, part, sems.at[len(copies)]))
        copies[-1].start()
    for far in blocks_far:
        rows = far.shape[0]
        part = moving_ref.at[pl.ds(used, rows)]
        copies.append(pltpu.make_async_copy(far, part, sems.at[len(copies)]))
        copies[-1].start()
        used += rows
    for copy in copies:
        copy.wait()
    resident, moving = resident_ref[...], moving_ref[...]
    logits = dot(resident, moving, 1, 1) * scale_ref[0] + bias_ref[0]
    total = dot(jax.nn.sigmoid(logits).astype(BF), moving)
    own_rows, partner_rows = mine_ref.shape[0], blocks_far[0].shape[0]
    images, texts = (partner_rows, own_rows) if turned else (own_rows, partner_rows)
    hits = jnp.where(targets_ref[...] == iota((images, texts), 0), 1.0, 0.0)
    hits = hits.T if turned else hits
    mine_ref[...] = total[:own_rows] - dot(hits.astype(BF), moving_ref[:partner_rows])
    rest_ref[...] = total[own_rows:].astype(BF)
    outs = [
        pltpu.make_async_copy(mine_ref, mine_far, sems.at[len(copies)]),
        pltpu.make_async_copy(rest_ref, rest_far, sems.at[len(copies) + 1]),
    ]
    for copy in outs:
        copy.start()
    for copy in outs:
        copy.wait()


def pair_call(turned, name, scalars, targets, own, other, blocks, after):
    rows, width = own.shape
    moving = (sum(block.shape[0] for block in blocks), width)
    arrays = [targets, own, other, *blocks]
    return pl.pallas_call(
        functools.partial(pair_sums, turned, len(blocks)),
        out_shape=[jax.ShapeDtypeStruct((rows, width), d) for d in (F32, BF)],
        in_specs=[SMEM] * 2 + [FAR] * (len(arrays) + len(after)),
        out_specs=[FAR] * 2,
        scratch_shapes=[
            pltpu.VMEM(targets.shape, targets.dtype),
            pltpu.VMEM((2 * rows, width), BF),
            pltpu.VMEM(moving, BF),
            pltpu.VMEM((rows, width), F32),
            pltpu.VMEM((rows, width), BF),
            pltpu.SemaphoreType.DMA((len(arrays) + 2,)),
        ],
        compiler_params=pltpu.CompilerParams(vmem_limit_bytes=64 * 2**20),
        name=name,
    )(*scalars, *arrays, *after)


def image_back(scale_ref, mine_ref, rest_ref, owners_ref, out_ref):
    gradient = (scale_ref[0] * (mine_ref[...] + rest_ref[...].astype(F32))).astype(BF)
    out_ref[...] = dot(requested(owners_ref, True), gradient).astype(BF).reshape(out_ref.shape)


def both_back(
    scale_ref, mine_ref, rest_ref, text_unit_ref, text_norm_ref,
    received_ref, select_ref, pool_unit_ref, pool_norm_ref,
    text_grad_ref, pool_grad_ref, strips_ref,
):
    columns, _, strip, rows = strips_ref.shape
    gradient = scale_ref[0] * (mine_ref[...] + rest_ref[...].astype(F32))
    gradient = pull_back(text_unit_ref[...], text_norm_ref[...], gradient)
    text_grad_ref[...] = gradient.astype(BF)
    strips_ref[:, 0] = gradient.T.astype(BF).reshape(columns, strip, rows)

    received = received_ref[...].reshape(select_ref.shape[0], -1)
    choose = select_ref[...].astype(F32).T.astype(BF)
    gradient = pull_back(pool_unit_ref[...], pool_norm_ref[...], dot(choose, received))
    pool_grad_ref[...] = gradient.astype(BF)
    strips_ref[:, 1] = gradient.T.astype(BF).reshape(columns, strip, rows)


def head_terms(strips_ref, *refs):
    x, yhi, core = (lax.axis_index(axis) for axis in REP_AXES)
    *feats_refs, out_ref = refs
    _, strip, lanes = strips_ref.shape
    extra = strip - lanes
    terms = jnp.zeros((2 * lanes, feats_refs[0].shape[1]), F32)
    for i, feats_ref in enumerate(feats_refs):
        along, across = (0, 3, 1, 2)[i // 2], i % 2
        blocks = []
        for dc in range(2):
            source = lax.rem(x + along, 4) * 4 + lax.rem(yhi + across, 2) * 2 + lax.rem(core + dc, 2)
            blocks.append(strips_ref[source])
        block = jnp.concatenate(blocks, axis=1)
        block = jnp.concatenate([block[:lanes]] + [block[lanes:]] * (lanes // extra), axis=0)
        terms += dot(block, feats_ref[...])
    turned = terms.T
    turned = jnp.concatenate([turned, jnp.zeros((8, 2 * lanes), F32)], axis=0)
    row, lane = iota((8, lanes), 0), iota((8, lanes), 1)
    diagonal = (lax.div(lane, extra) == row) & (row < 5)
    for pair in range(out_ref.shape[0]):
        halves = []
        for start in (9 * pair, 9 * pair + 4):
            last = jnp.where(diagonal, turned[start : start + 8, lanes:], 0.0)
            last = jnp.sum(last, axis=0, keepdims=True)
            main = turned[start : start + 8, :lanes]
            halves.append(jnp.where(row < 5, main, jnp.where(row == 5, last, 0.0)))
        out_ref[pair] = jnp.concatenate(halves, axis=0).astype(BF)


def head_sums(terms_ref, out_ref):
    core = lax.axis_index("core")
    lanes = terms_ref.shape[2]
    extra = out_ref.shape[1] // 8 - lanes
    row, lane = iota((16, lanes), 0), iota((16, lanes), 1)
    diagonal = lax.div(lane, extra) == lax.rem(row, 8)
    fold = jnp.where(lax.rem(iota((lanes, extra), 0), extra) == iota((lanes, extra), 1), 1.0, 0.0)
    strips = []
    for k in range(8):
        total = terms_ref[k].astype(F32)
        for i in range(1, 16):
            total += terms_ref[8 * i + k].astype(F32)
        last = jnp.where(row < 8, total[5:6], total[13:14])
        last = jnp.where(diagonal, last, 0.0)
        last = jnp.dot(last, fold, preferred_element_type=F32, precision=lax.Precision.HIGHEST)
        strips += [total, last]
    rows = jnp.concatenate(strips, axis=1)
    to, source = iota((16, 16), 0), iota((16, 16), 1)
    order = jnp.where(2 * lax.rem(source, 8) + lax.div(source, 8) == to + core, 1.0, 0.0)
    rows = jnp.dot(order, rows, preferred_element_type=F32, precision=lax.Precision.HIGHEST)
    out_ref[...] = rows[: out_ref.shape[0]]


def per_device(
    caption_feats,
    text_head,
    image_pool,
    image_head,
    image_owner,
    image_slot,
    caption_image,
    logit_scale,
    logit_bias,
):
    captions = caption_feats[0]
    pool = image_pool[0]
    owners = image_owner[:, :, 0]
    groups, images = owners.shape
    texts, width = captions.shape
    pool_rows = pool.shape[0]
    outs = [
        ((pool_rows, width), F32),
        ((pool_rows, 1), F32),
        ((groups, SLOTS, width), BF),
        ((groups * SLOTS, pool_rows), BF),
        ((texts, width), F32),
        ((texts, 1), F32),
        ((texts, width), BF),
        ((texts, width), BF),
        ((texts, width), BF),
    ]
    arrays = [owners, image_slot, pool, image_head, captions, text_head]
    pool_unit, pool_norm, outgoing, select, text_unit, text_norm, text_emb, keep, give = pl.pallas_call(
        front,
        out_shape=[jax.ShapeDtypeStruct(s, d) for s, d in outs],
        in_specs=[FAR] * len(arrays),
        out_specs=[FAR] * len(outs),
        scratch_shapes=[pltpu.VMEM(s, d) for s, d in [(a.shape, a.dtype) for a in arrays] + outs]
        + [pltpu.SemaphoreType.DMA((19,))],
        compiler_params=pltpu.CompilerParams(vmem_limit_bytes=64 * 2**20),
        name="front",
    )(*arrays)
    text_blocks = gathered_along_z(text_emb, 1)
    arrived = lax.all_to_all(outgoing, REP_AXES, 0, 0, tiled=True)
    other_text = shifted(text_emb, "ylo", 1)
    given = shifted(give, "core", 1)
    far_keep = shifted(keep, "yhi", 1)
    far_given = lax.ppermute(give, ("yhi", "core"), [(i, 3 - i) for i in range(4)])
    (image_emb,) = call(
        arrive, [((images, width), BF)], "arrive", [], [arrived, owners], [given]
    )
    other_image = shifted(image_emb, "ylo", 1)
    image_blocks = [image_emb]
    ahead = behind = image_emb
    for step in range(3):
        ahead, behind = shifted(ahead, "z", -1), shifted(behind, "z", 1)
        ahead, behind = together(ahead, behind)
        image_blocks += [ahead, behind]
    image_blocks += [shifted(ahead, "z", -1)]
    home, far = call(
        joined, [((2 * texts, width), BF)] * 2, "joined", [], [keep, given, far_keep, far_given],
    )
    feats = [home, far]
    feats += [shifted(home, "x", 1), shifted(far, "x", 1)]
    feats += [shifted(home, "x", -1), shifted(far, "x", -1)]
    feats += [shifted(feats[2], "x", 1), shifted(feats[5], "x", -1)]

    scalars = [logit_scale, logit_bias]
    image_mine, image_rest = pair_call(
        False, "image_sums", scalars, caption_image, image_emb, other_image, text_blocks, [home]
    )
    image_sent, image_rest = image_rest, shifted(image_rest, "ylo", 1)
    (send_back,) = call(
        image_back, [((groups, SLOTS, width), BF)], "image_back",
        [logit_scale], [image_mine, image_rest, owners],
        [feats[2], feats[4], *image_blocks[6:]],
    )
    received = lax.all_to_all(send_back, REP_AXES, 0, 0, tiled=True)

    text_mine, text_rest = pair_call(
        True, "text_sums", scalars, caption_image, text_emb, other_text, image_blocks,
        [send_back],
    )
    text_rest = shifted(text_rest, "ylo", 1)
    columns = groups // 2
    strip = width // columns
    text_grad, pool_proj_grad, strips = call(
        both_back,
        [((texts, width), BF), ((pool_rows, width), BF), ((columns, 2, strip, texts), BF)],
        "both_back", scalars[:1],
        [text_mine, text_rest, text_unit, text_norm, received, select, pool_unit, pool_norm],
        [feats[3], feats[5]],
    )
    strips = lax.all_to_all(strips.reshape(groups, strip, texts), REP_AXES, 0, 0, tiled=True)
    text_feat_grad = dot(text_grad, text_head, 1, 1).astype(BF)
    pool_grad = dot(pool_proj_grad, image_head, 1, 1).astype(BF)

    (terms,) = call(
        head_terms, [((128, 16, 128), BF)], "head_terms", [],
        [strips, *feats],
    )
    terms = lax.all_to_all(terms.reshape(256, 8, 128), CAP_AXES + REP_AXES, 0, 0, tiled=True)
    (head_share,) = call(
        head_sums, [((9, width), F32)], "head_sums", [], [terms.reshape(128, 16, 128)]
    )
    return text_feat_grad[None], pool_grad[None], head_share


def solution(mesh):
    fine = Mesh(mesh.devices.reshape(2, 8, 4, 2, 2), CAP_AXES + REP_AXES)
    in_specs = (
        P(REP_AXES, CAP_AXES, None),
        P(),
        P(CAP_AXES, REP_AXES, None),
        P(),
        P(None, CAP_AXES, None),
        P(None, CAP_AXES),
        P(REP_AXES, CAP_AXES),
        P(),
        P(),
    )
    out_specs = (
        P(REP_AXES, CAP_AXES, None),
        P(CAP_AXES, REP_AXES, None),
        P(CAP_AXES + REP_AXES, None),
    )
    return jax.shard_map(
        per_device, mesh=fine, in_specs=in_specs, out_specs=out_specs, check_vma=False
    )
```

```python
import functools

import jax
import jax.numpy as jnp
from jax import lax
from jax.experimental import pallas as pl
from jax.experimental.pallas import tpu as pltpu
from jax.sharding import Mesh
from jax.sharding import PartitionSpec as P

BF = jnp.bfloat16
F32 = jnp.float32
CAP_AXES = ("ylo", "z")
REP_AXES = ("x", "yhi", "core")
SLOTS = 16
FAR = pl.BlockSpec(memory_space=pltpu.HBM)
SMEM = pl.BlockSpec(memory_space=pltpu.SMEM)


def shifted(block, axis, distance):
    size = lax.axis_size(axis)
    return lax.ppermute(block, axis, [(i, (i + distance) % size) for i in range(size)])


def gathered_along_z(block, way):
    ahead, behind, found = block, block, [block]
    for _ in range(3):
        ahead, behind = shifted(ahead, "z", way), shifted(behind, "z", -way)
        found += [ahead, behind]
    return found + [shifted(ahead, "z", way)]


def together(*arrays):
    return lax.optimization_barrier(arrays)


def call(body, outs, name, scalars, arrays, after=()):
    shapes = [jax.ShapeDtypeStruct(shape, dtype) for shape, dtype in outs]
    count, total = len(arrays), len(arrays) + len(outs)

    def kernel(*refs):
        head = refs[: len(scalars)]
        far = refs[len(scalars) :][:count] + refs[len(scalars) + count + len(after) :][: len(outs)]
        near = refs[len(scalars) + len(after) + total : -1]
        sems = refs[-1]
        copies = [
            pltpu.make_async_copy(far[i], near[i], sems.at[i])
            if i < count
            else pltpu.make_async_copy(near[i], far[i], sems.at[i])
            for i in range(total)
        ]
        for i in range(count):
            copies[i].start()
        for i in range(count):
            copies[i].wait()
        body(*head, *near)
        for i in range(count, total):
            copies[i].start()
        for i in range(count, total):
            copies[i].wait()

    everything = [(a.shape, a.dtype) for a in arrays] + list(outs)
    return pl.pallas_call(
        kernel,
        out_shape=shapes,
        in_specs=[SMEM] * len(scalars) + [FAR] * (count + len(after)),
        out_specs=[FAR] * len(outs),
        scratch_shapes=[pltpu.VMEM(s, d) for s, d in everything]
        + [pltpu.SemaphoreType.DMA((total,))],
        compiler_params=pltpu.CompilerParams(vmem_limit_bytes=64 * 2**20),
        name=name,
    )(*scalars, *arrays, *after)


def dot(a, b, left=1, right=0):
    return lax.dot_general(a, b, (((left,), (right,)), ((), ())), preferred_element_type=F32)


def iota(shape, dim):
    return lax.broadcasted_iota(jnp.int32, shape, dim)


def one_hot(condition):
    return jnp.where(condition, 1.0, 0.0).astype(BF)


def pull_back(unit, norm, gradient):
    radial = jnp.sum(unit * gradient, axis=-1, keepdims=True)
    return (gradient - unit * radial) / norm


def front(
    owners_far, slots_far, pool_far, image_head_far, captions_far, text_head_far,
    pool_unit_far, pool_norm_far, out_far, select_far, text_unit_far, text_norm_far, emb_far,
    keep_far, give_far,
    owners_ref, slots_ref, pool_ref, image_head_ref, captions_ref, text_head_ref,
    pool_unit_ref, pool_norm_ref, out_ref, select_ref, text_unit_ref, text_norm_ref, emb_ref,
    keep_ref, give_ref, sems,
):
    width = pool_ref.shape[1]
    depth = width // 3
    used = [0]

    def moved(source, target):
        copy = pltpu.make_async_copy(source, target, sems.at[used[0]])
        used[0] += 1
        copy.start()
        return copy

    def cut(far, ref):
        rows = [pl.ds(i * depth, depth) for i in range(3)]
        return [moved(far.at[r], ref.at[r]) for r in rows]

    small = [moved(owners_far, owners_ref), moved(slots_far, slots_ref)]
    pool_in = moved(pool_far, pool_ref)
    image_head_in = cut(image_head_far, image_head_ref)
    captions_in = moved(captions_far, captions_ref)
    text_head_in = cut(text_head_far, text_head_ref)

    def projected(feats_ref, head_ref, head_in):
        total = jnp.zeros((feats_ref.shape[0], width), F32)
        for i in range(3):
            head_in[i].wait()
            rows = pl.ds(i * depth, depth)
            total += dot(feats_ref[:, rows], head_ref[rows])
        norm = jnp.sqrt(jnp.sum(total * total, axis=-1, keepdims=True) + 1e-06)
        return total / norm, norm

    for copy in small:
        copy.wait()
    owners = owners_ref[...]
    groups, images = owners.shape
    rows = groups * SLOTS
    owned = owners == lax.axis_index(REP_AXES)
    place = dot(one_hot(owned), one_hot(iota((images, images), 0) < iota((images, images), 1)))
    code = jnp.where(owned, place, -1.0)
    spread = one_hot(lax.div(iota((rows, groups), 0), SLOTS) == iota((rows, groups), 1))
    code_rows = dot(spread, code.astype(BF))
    slot_rows = dot(spread, slots_ref[...].astype(F32).astype(BF))
    at = lax.rem(iota((rows, images), 0), SLOTS).astype(F32)
    slot = jnp.sum(jnp.where(code_rows == at, slot_rows + 1.0, 0.0), axis=1, keepdims=True) - 1.0
    select = one_hot(slot == iota((rows, pool_ref.shape[0]), 1).astype(F32))
    select_ref[...] = select
    outs = [moved(select_ref, select_far)]

    pool_in.wait()
    unit, norm = projected(pool_ref, image_head_ref, image_head_in)
    pool_unit_ref[...] = unit
    pool_norm_ref[...] = norm
    out_ref[...] = dot(select, unit.astype(BF)).astype(BF).reshape(out_ref.shape)
    outs += [
        moved(out_ref, out_far),
        moved(pool_unit_ref, pool_unit_far),
        moved(pool_norm_ref, pool_norm_far),
    ]

    captions_in.wait()
    first = lax.axis_index("core") == 0
    keep_ref[...] = jnp.where(first, captions_ref[...], pool_ref[...])
    give_ref[...] = jnp.where(first, pool_ref[...], captions_ref[...])
    outs += [moved(keep_ref, keep_far), moved(give_ref, give_far)]
    unit, norm = projected(captions_ref, text_head_ref, text_head_in)
    emb_ref[...] = unit.astype(BF)
    outs += [moved(emb_ref, emb_far)]
    text_unit_ref[...] = unit
    text_norm_ref[...] = norm
    outs += [moved(text_unit_ref, text_unit_far), moved(text_norm_ref, text_norm_far)]
    for copy in outs:
        copy.wait()


def requested(owners_ref, turned):
    owners = owners_ref[...]
    groups, images = owners.shape
    row, lane = iota((images, images), 0), iota((images, images), 1)
    mine = jnp.sum(
        jnp.where(iota((groups, images), 0) == lax.axis_index(REP_AXES), owners.astype(F32), 0.0),
        axis=0,
        keepdims=True,
    )
    mine_t = jnp.sum(jnp.where(row == lane, mine, 0.0), axis=1, keepdims=True)
    same = mine == mine_t
    if turned:
        before = jnp.sum(jnp.where(same & (row < lane), 1.0, 0.0), axis=0, keepdims=True)
        rows = iota((groups * SLOTS, images), 0)
        return one_hot(mine * SLOTS + before == rows.astype(F32))
    before = jnp.sum(jnp.where(same & (lane < row), 1.0, 0.0), axis=1, keepdims=True)
    return one_hot(mine_t * SLOTS + before == iota((images, groups * SLOTS), 1).astype(F32))


def arrive(arrived_ref, owners_ref, emb_ref):
    hit = requested(owners_ref, False)
    emb_ref[...] = dot(hit, arrived_ref[...].reshape(hit.shape[1], -1)).astype(BF)


def joined(a_ref, b_ref, c_ref, d_ref, ab_ref, cd_ref):
    rows = a_ref.shape[0]
    ab_ref[:rows] = a_ref[...]
    ab_ref[rows:] = b_ref[...]
    cd_ref[:rows] = c_ref[...]
    cd_ref[rows:] = d_ref[...]


def pair_sums(turned, count, scale_ref, bias_ref, targets_far, own_far, other_far, *refs):
    blocks_far = refs[:count]
    mine_far, rest_far, targets_ref, resident_ref, moving_ref, mine_ref, rest_ref, sems = refs[-8:]
    used = 0
    copies = []
    for far, ref in ((own_far, resident_ref), (other_far, resident_ref), (targets_far, targets_ref)):
        part = ref.at[pl.ds(own_far.shape[0], own_far.shape[0])] if far is other_far else ref
        part = ref.at[pl.ds(0, own_far.shape[0])] if far is own_far else part
        copies.append(pltpu.make_async_copy(far, part, sems.at[len(copies)]))
        copies[-1].start()
    for far in blocks_far:
        rows = far.shape[0]
        part = moving_ref.at[pl.ds(used, rows)]
        copies.append(pltpu.make_async_copy(far, part, sems.at[len(copies)]))
        copies[-1].start()
        used += rows
    for copy in copies:
        copy.wait()
    resident, moving = resident_ref[...], moving_ref[...]
    logits = dot(resident, moving, 1, 1) * scale_ref[0] + bias_ref[0]
    total = dot(jax.nn.sigmoid(logits).astype(BF), moving)
    own_rows, partner_rows = mine_ref.shape[0], blocks_far[0].shape[0]
    images, texts = (partner_rows, own_rows) if turned else (own_rows, partner_rows)
    hits = jnp.where(targets_ref[...] == iota((images, texts), 0), 1.0, 0.0)
    hits = hits.T if turned else hits
    mine_ref[...] = total[:own_rows] - dot(hits.astype(BF), moving_ref[:partner_rows])
    rest_ref[...] = total[own_rows:].astype(BF)
    outs = [
        pltpu.make_async_copy(mine_ref, mine_far, sems.at[len(copies)]),
        pltpu.make_async_copy(rest_ref, rest_far, sems.at[len(copies) + 1]),
    ]
    for copy in outs:
        copy.start()
    for copy in outs:
        copy.wait()


def pair_call(turned, name, scalars, targets, own, other, blocks, after):
    rows, width = own.shape
    moving = (sum(block.shape[0] for block in blocks), width)
    arrays = [targets, own, other, *blocks]
    return pl.pallas_call(
        functools.partial(pair_sums, turned, len(blocks)),
        out_shape=[jax.ShapeDtypeStruct((rows, width), d) for d in (F32, BF)],
        in_specs=[SMEM] * 2 + [FAR] * (len(arrays) + len(after)),
        out_specs=[FAR] * 2,
        scratch_shapes=[
            pltpu.VMEM(targets.shape, targets.dtype),
            pltpu.VMEM((2 * rows, width), BF),
            pltpu.VMEM(moving, BF),
            pltpu.VMEM((rows, width), F32),
            pltpu.VMEM((rows, width), BF),
            pltpu.SemaphoreType.DMA((len(arrays) + 2,)),
        ],
        compiler_params=pltpu.CompilerParams(vmem_limit_bytes=64 * 2**20),
        name=name,
    )(*scalars, *arrays, *after)


def image_back(scale_ref, mine_ref, rest_ref, owners_ref, out_ref):
    gradient = (scale_ref[0] * (mine_ref[...] + rest_ref[...].astype(F32))).astype(BF)
    out_ref[...] = dot(requested(owners_ref, True), gradient).astype(BF).reshape(out_ref.shape)


def both_back(
    scale_ref, mine_ref, rest_ref, text_unit_ref, text_norm_ref,
    received_ref, select_ref, pool_unit_ref, pool_norm_ref,
    text_grad_ref, pool_grad_ref, strips_ref,
):
    columns, _, strip, rows = strips_ref.shape
    gradient = scale_ref[0] * (mine_ref[...] + rest_ref[...].astype(F32))
    gradient = pull_back(text_unit_ref[...], text_norm_ref[...], gradient)
    text_grad_ref[...] = gradient.astype(BF)
    strips_ref[:, 0] = gradient.T.astype(BF).reshape(columns, strip, rows)

    received = received_ref[...].reshape(select_ref.shape[0], -1)
    choose = select_ref[...].astype(F32).T.astype(BF)
    gradient = pull_back(pool_unit_ref[...], pool_norm_ref[...], dot(choose, received))
    pool_grad_ref[...] = gradient.astype(BF)
    strips_ref[:, 1] = gradient.T.astype(BF).reshape(columns, strip, rows)


def head_terms(strips_ref, *refs):
    x, yhi, core = (lax.axis_index(axis) for axis in REP_AXES)
    *feats_refs, out_ref = refs
    _, strip, lanes = strips_ref.shape
    extra = strip - lanes
    terms = jnp.zeros((2 * lanes, feats_refs[0].shape[1]), F32)
    for i, feats_ref in enumerate(feats_refs):
        along, across = (0, 3, 1, 2)[i // 2], i % 2
        blocks = []
        for dc in range(2):
            source = lax.rem(x + along, 4) * 4 + lax.rem(yhi + across, 2) * 2 + lax.rem(core + dc, 2)
            blocks.append(strips_ref[source])
        block = jnp.concatenate(blocks, axis=1)
        block = jnp.concatenate([block[:lanes]] + [block[lanes:]] * (lanes // extra), axis=0)
        terms += dot(block, feats_ref[...])
    turned = terms.T
    turned = jnp.concatenate([turned, jnp.zeros((8, 2 * lanes), F32)], axis=0)
    row, lane = iota((8, lanes), 0), iota((8, lanes), 1)
    diagonal = (lax.div(lane, extra) == row) & (row < 5)
    for pair in range(out_ref.shape[0]):
        halves = []
        for start in (9 * pair, 9 * pair + 4):
            last = jnp.where(diagonal, turned[start : start + 8, lanes:], 0.0)
            last = jnp.sum(last, axis=0, keepdims=True)
            main = turned[start : start + 8, :lanes]
            halves.append(jnp.where(row < 5, main, jnp.where(row == 5, last, 0.0)))
        out_ref[pair] = jnp.concatenate(halves, axis=0).astype(BF)


def head_sums(terms_ref, out_ref):
    core = lax.axis_index("core")
    lanes = terms_ref.shape[2]
    extra = out_ref.shape[1] // 8 - lanes
    row, lane = iota((16, lanes), 0), iota((16, lanes), 1)
    diagonal = lax.div(lane, extra) == lax.rem(row, 8)
    fold = jnp.where(lax.rem(iota((lanes, extra), 0), extra) == iota((lanes, extra), 1), 1.0, 0.0)
    strips = []
    for k in range(8):
        total = terms_ref[k].astype(F32)
        for i in range(1, 16):
            total += terms_ref[8 * i + k].astype(F32)
        last = jnp.where(row < 8, total[5:6], total[13:14])
        last = jnp.where(diagonal, last, 0.0)
        last = jnp.dot(last, fold, preferred_element_type=F32, precision=lax.Precision.HIGHEST)
        strips += [total, last]
    rows = jnp.concatenate(strips, axis=1)
    to, source = iota((16, 16), 0), iota((16, 16), 1)
    order = jnp.where(2 * lax.rem(source, 8) + lax.div(source, 8) == to + core, 1.0, 0.0)
    rows = jnp.dot(order, rows, preferred_element_type=F32, precision=lax.Precision.HIGHEST)
    out_ref[...] = rows[: out_ref.shape[0]]


def per_device(
    caption_feats,
    text_head,
    image_pool,
    image_head,
    image_owner,
    image_slot,
    caption_image,
    logit_scale,
    logit_bias,
):
    captions = caption_feats[0]
    pool = image_pool[0]
    owners = image_owner[:, :, 0]
    groups, images = owners.shape
    texts, width = captions.shape
    pool_rows = pool.shape[0]
    outs = [
        ((pool_rows, width), F32),
        ((pool_rows, 1), F32),
        ((groups, SLOTS, width), BF),
        ((groups * SLOTS, pool_rows), BF),
        ((texts, width), F32),
        ((texts, 1), F32),
        ((texts, width), BF),
        ((texts, width), BF),
        ((texts, width), BF),
    ]
    arrays = [owners, image_slot, pool, image_head, captions, text_head]
    pool_unit, pool_norm, outgoing, select, text_unit, text_norm, text_emb, keep, give = pl.pallas_call(
        front,
        out_shape=[jax.ShapeDtypeStruct(s, d) for s, d in outs],
        in_specs=[FAR] * len(arrays),
        out_specs=[FAR] * len(outs),
        scratch_shapes=[pltpu.VMEM(s, d) for s, d in [(a.shape, a.dtype) for a in arrays] + outs]
        + [pltpu.SemaphoreType.DMA((19,))],
        compiler_params=pltpu.CompilerParams(vmem_limit_bytes=64 * 2**20),
        name="front",
    )(*arrays)
    text_blocks = gathered_along_z(text_emb, 1)
    arrived = lax.all_to_all(outgoing, REP_AXES, 0, 0, tiled=True)
    other_text = shifted(text_emb, "ylo", 1)
    given = shifted(give, "core", 1)
    far_keep = shifted(keep, "yhi", 1)
    far_given = lax.ppermute(give, ("yhi", "core"), [(i, 3 - i) for i in range(4)])
    (image_emb,) = call(
        arrive, [((images, width), BF)], "arrive", [], [arrived, owners], [given]
    )
    other_image = shifted(image_emb, "ylo", 1)
    image_blocks = [image_emb]
    ahead = behind = image_emb
    for step in range(3):
        ahead, behind = shifted(ahead, "z", -1), shifted(behind, "z", 1)
        ahead, behind = together(ahead, behind)
        image_blocks += [ahead, behind]
    image_blocks += [shifted(ahead, "z", -1)]
    home, far = call(
        joined, [((2 * texts, width), BF)] * 2, "joined", [], [keep, given, far_keep, far_given],
    )
    feats = [home, far]
    feats += [shifted(home, "x", 1), shifted(far, "x", 1)]
    feats += [shifted(home, "x", -1), shifted(far, "x", -1)]
    feats += [shifted(feats[2], "x", 1), shifted(feats[5], "x", -1)]

    scalars = [logit_scale, logit_bias]
    image_mine, image_rest = pair_call(
        False, "image_sums", scalars, caption_image, image_emb, other_image, text_blocks, [home]
    )
    image_sent, image_rest = image_rest, shifted(image_rest, "ylo", 1)
    (send_back,) = call(
        image_back, [((groups, SLOTS, width), BF)], "image_back",
        [logit_scale], [image_mine, image_rest, owners],
        [home, *image_blocks[6:]],
    )
    received = lax.all_to_all(send_back, REP_AXES, 0, 0, tiled=True)

    text_mine, text_rest = pair_call(
        True, "text_sums", scalars, caption_image, text_emb, other_text, image_blocks,
        [send_back, feats[2], feats[4]],
    )
    text_rest = shifted(text_rest, "ylo", 1)
    columns = groups // 2
    strip = width // columns
    text_grad, pool_proj_grad, strips = call(
        both_back,
        [((texts, width), BF), ((pool_rows, width), BF), ((columns, 2, strip, texts), BF)],
        "both_back", scalars[:1],
        [text_mine, text_rest, text_unit, text_norm, received, select, pool_unit, pool_norm],
        [feats[3], feats[5]],
    )
    strips = lax.all_to_all(strips.reshape(groups, strip, texts), REP_AXES, 0, 0, tiled=True)
    text_feat_grad = dot(text_grad, text_head, 1, 1).astype(BF)
    pool_grad = dot(pool_proj_grad, image_head, 1, 1).astype(BF)

    (terms,) = call(
        head_terms, [((128, 16, 128), BF)], "head_terms", [],
        [strips, *feats],
    )
    terms = lax.all_to_all(terms.reshape(256, 8, 128), CAP_AXES + REP_AXES, 0, 0, tiled=True)
    (head_share,) = call(
        head_sums, [((9, width), F32)], "head_sums", [], [terms.reshape(128, 16, 128)]
    )
    return text_feat_grad[None], pool_grad[None], head_share


def solution(mesh):
    fine = Mesh(mesh.devices.reshape(2, 8, 4, 2, 2), CAP_AXES + REP_AXES)
    in_specs = (
        P(REP_AXES, CAP_AXES, None),
        P(),
        P(CAP_AXES, REP_AXES, None),
        P(),
        P(None, CAP_AXES, None),
        P(None, CAP_AXES),
        P(REP_AXES, CAP_AXES),
        P(),
        P(),
    )
    out_specs = (
        P(REP_AXES, CAP_AXES, None),
        P(CAP_AXES, REP_AXES, None),
        P(CAP_AXES + REP_AXES, None),
    )
    return jax.shard_map(
        per_device, mesh=fine, in_specs=in_specs, out_specs=out_specs, check_vma=False
    )
```
